256 devices in a mesh: rep: 16 (over y, x_lo, core), exp: 16 (over z, x_hi).
Axes of the slice: x: 4 (x_hi: 2, x_lo: 2; x = x_hi * 2 + x_lo), y: 4, z: 8, core: 2. Of those that a mesh axis runs over, the one named last changes fastest.
Arguments:
- acts: bfloat16 [16, 16, 64, 2, 2048], P('rep', 'exp'), may hold values from -6 to 6
- cotangent: bfloat16 [16, 64, 2, 32, 768], P('rep', 'exp'), may hold values from -0.25 to 0.25
- counts: int32 [16, 16, 64], P('rep', 'exp'), may hold values from 1 to 2, as said below
- momentum: bfloat16 [2048, 64, 2, 768], P('rep', 'exp'), may hold values from -24 to 24
Outputs:
- new_momentum: bfloat16 [2048, 64, 2, 768], P('rep', 'exp')
- update: bfloat16 [2048, 64, 2, 768], P('rep', 'exp')
The draws below stay inside these ranges and needn't reach their ends.
Inputs may be any that keep to these rules, and one draw needn't show every extreme that they name: `counts`: in every draw some source device sends exactly 2 tokens to some expert.
All inputs are finite; a program needn't handle non-finite values.
Results may differ from the reference program's by a relative error of at most 0.02.
Values may be sent and summed in bfloat16 or wider, within the bound.
A program may use at most 128 MiB of HBM per device.

```python
import math
import jax
import jax.numpy as jnp
from jax import lax

D = 2048
FF = 768
CAPS = 2
ITERS = 2
REPLICAS = 16
GROUPS = 16
EXPERTS = 64
ROWS = 32


def draw_counts(key, part):
    key = jax.random.fold_in(key, 7)
    first_key, second_key = jax.random.split(key)
    shape_all = (REPLICAS, GROUPS, EXPERTS)
    drawn = jax.random.randint(first_key, shape_all, 1, CAPS + 1)
    flat_index = lax.broadcasted_iota(jnp.int32, shape_all, 0) * (GROUPS * EXPERTS) + lax.broadcasted_iota(jnp.int32, shape_all, 1) * EXPERTS + lax.broadcasted_iota(jnp.int32, shape_all, 2)
    chosen = jax.random.randint(second_key, (), 0, REPLICAS * GROUPS * EXPERTS)
    return jnp.where(flat_index == chosen, CAPS, drawn).astype(jnp.int32)


def draw_momentum(key, part):
    key = jax.random.fold_in(key, 11)
    value_key, half_key = jax.random.split(key)
    shape_all = (D, EXPERTS, 2, FF)
    base = jnp.clip(jax.random.normal(value_key, shape_all, jnp.float32), -6.0, 6.0)
    shard_len = D // REPLICAS
    row_pos = lax.broadcasted_iota(jnp.int32, (D,), 0)
    heavy_half = jax.random.randint(half_key, (REPLICAS,), 0, 2)
    second_half = (row_pos % shard_len >= shard_len // 2).astype(jnp.int32)
    heavy = second_half == heavy_half[row_pos // shard_len]
    row_scale = jnp.where(heavy, 4.0, 1.0).astype(jnp.float32)
    return (base * row_scale[:, None, None, None]).astype(jnp.bfloat16)


def block_scale(key, extent, shards, low, largest):
    gain = 1.0
    for axis_at, blocks in shards:
        draws = jax.random.uniform(jax.random.fold_in(jax.random.fold_in(key, 6), axis_at), (blocks,), jnp.float32, low / len(shards), largest / len(shards))
        gain = gain * jnp.repeat(jnp.exp(draws), extent[axis_at] // blocks).reshape((-1,) + (1,) * (len(extent) - 1 - axis_at))
    return gain


def gaussian(key, dims, spread, most, cuts=(), dtype=jnp.bfloat16):
    gain = block_scale(key, dims, cuts, -0.22, 0.18) if cuts else 1.0
    result = jax.random.normal(key, dims, jnp.float32) * spread * gain
    return jnp.minimum(jnp.maximum(result, -most), most).astype(dtype)


def setup_inputs(seed: int = 0) -> dict:
    streams_of = jax.random.split(jax.random.key(seed), 5)
    acts = gaussian(streams_of[0], (REPLICAS, GROUPS, EXPERTS, CAPS, D), 1.0, 6.0, ((0, 16), (1, 16)))
    cotangent = gaussian(streams_of[1], (REPLICAS, EXPERTS, 2, ROWS, FF), (REPLICAS * ROWS) ** -0.5, 0.25, ((0, 16), (1, 16)))
    counts = draw_counts(jax.random.fold_in(streams_of[4], 71), 0)
    momentum = draw_momentum(jax.random.fold_in(streams_of[4], 71), 0)
    return {"acts": acts, "cotangent": cotangent, "counts": counts, "momentum": momentum}


coef_a = 3.4445
coef_b = -4.775
coef_c = 2.0315
decay_rate = 0.95
norm_eps = 1e-07

def newton_schulz(matrix):
    values = matrix.astype(jnp.float32)
    ortho = (values / (jnp.sqrt(jnp.sum(values * values)) + norm_eps)).astype(jnp.bfloat16)
    ortho = lax.optimization_barrier(ortho)
    for sweep in range(ITERS):
        gram_mat = lax.optimization_barrier(jnp.dot(ortho.T, ortho, preferred_element_type=jnp.float32).astype(jnp.bfloat16))
        square = jnp.dot(gram_mat, gram_mat, preferred_element_type=jnp.float32)
        poly_mat = (coef_b * gram_mat.astype(jnp.float32) + coef_c * square).astype(jnp.bfloat16)
        ortho = (coef_a * ortho.astype(jnp.float32) + jnp.dot(ortho, poly_mat, preferred_element_type=jnp.float32)).astype(jnp.bfloat16)
        ortho = lax.optimization_barrier(ortho)
    return ortho

def one_expert(inputs):
    tokens, grads_out, mom_old = inputs

    def add_replica(running, pair):
        tok_rep, cot_rep = pair
        part = jnp.einsum('td,ktf->dkf', tok_rep.astype(jnp.float32), cot_rep.astype(jnp.float32))
        part = lax.optimization_barrier(part.astype(jnp.bfloat16)).astype(jnp.float32)
        return (running + part, None)
    grad, unused = lax.scan(add_replica, jnp.zeros((D, 2, FF), jnp.float32), (tokens, grads_out))
    mom_new = decay_rate * mom_old.astype(jnp.float32) + grad
    nest = (grad + decay_rate * mom_new).astype(jnp.bfloat16)
    results = [newton_schulz(nest[:, kind, :]) for kind in range(2)]
    ortho = jnp.stack(results, axis=1)
    update = (math.sqrt(D) * ortho.astype(jnp.float32)).astype(jnp.bfloat16)
    return (mom_new.astype(jnp.bfloat16), update)

def reference(acts, cotangent, counts, momentum):
    slot_index = lax.broadcasted_iota(jnp.int32, (1, 1, 1, CAPS, 1), 3)
    live_rows = slot_index < counts[:, :, :, None, None]
    live = jnp.where(live_rows, acts, jnp.zeros_like(acts))
    tokens = jnp.moveaxis(live, 2, 0).reshape(EXPERTS, REPLICAS, ROWS, D)
    grads_out = jnp.moveaxis(cotangent, 1, 0)
    mom_all = jnp.moveaxis(momentum, 1, 0)
    new_mom, update = lax.map(one_expert, (tokens, grads_out, mom_all))
    return (jnp.moveaxis(new_mom, 0, 1), jnp.moveaxis(update, 0, 1))
```

```python
import functools
import math

import jax
import jax.numpy as jnp
from jax import lax
from jax.experimental import pallas as pl
from jax.experimental.pallas import tpu as pltpu
from jax.sharding import PartitionSpec as P

coef_a = 3.4445
coef_b = -4.775
coef_c = 2.0315
decay_rate = 0.95
norm_eps = 1e-07

REP = 16
EXP = 16
CHIPS = 8
YS = 4
EXPERTS_HERE = 4
SLOTS = 2
WIDTH = 2048
HALF = WIDTH // 2
SHARD = 128
HIDDEN = 768
TOKENS = 32
TILE = 256

MESH = pl.DeviceIdType.MESH
f32 = jnp.float32
bf16 = jnp.bfloat16


def remote(src, dst, send_sem, recv_sem, rep, exp):
    return pltpu.make_async_remote_copy(
        src_ref=src,
        dst_ref=dst,
        send_sem=send_sem,
        recv_sem=recv_sem,
        device_id=(rep, exp),
        device_id_type=MESH,
    )


def dot32(left, right):
    return jnp.dot(left, right, preferred_element_type=f32)


def dot_rows(left, right):
    return lax.dot_general(left, right, (((0,), (0,)), ((), ())), preferred_element_type=f32)


def kernel(
    tok_in,
    cot_in,
    mom_in,
    new_out,
    upd_out,
    tok_r,
    t2_s,
    t2_r,
    cot_r,
    mom_r,
    new_s,
    nest_s,
    upd_s,
    gram_s,
    gram_r,
    gram_f,
    sq_s,
    sq_r,
    g0,
    bend0,
    step,
    g1,
    bend1,
    both,
    tok_ss,
    tok_rs,
    cot_ss,
    cot_rs,
    mom_ss,
    mom_rs,
    t2_ss,
    t2_rs,
    new_ss,
    new_rs,
    upd_ss,
    upd_rs,
    pair_ss,
    pair_rs,
    local_sem,
):
    rep = lax.axis_index("rep")
    exp = lax.axis_index("exp")
    chip = rep // 2
    core = lax.rem(rep, 2)
    y = rep // 4
    x = lax.rem(chip, 2)
    peer = y * 2 + core
    rep_x = y * 4 + (1 - x) * 2 + core
    rep_core = chip * 2 + (1 - core)

    def signal(to_rep, to_exp):
        pl.semaphore_signal(
            pltpu.get_barrier_semaphore(), inc=1, device_id=(to_rep, to_exp), device_id_type=MESH
        )

    def greet(i, carry):
        signal(rep, lax.rem(exp + i, EXP))
        signal(lax.rem(rep + i, REP), exp)
        signal(rep_x, lax.rem(exp + i, EXP))
        return carry

    lax.fori_loop(1, 16, greet, 0)
    pl.semaphore_wait(pltpu.get_barrier_semaphore(), 45)

    def tok_copy(i, other):
        to = lax.rem(exp + i, EXP)
        return remote(
            tok_in.at[to],
            tok_r.at[x, exp],
            tok_ss.at[other, i],
            tok_rs.at[x, exp],
            rep_x if other else rep,
            to,
        )

    def cot_copy(i):
        to = lax.rem(rep + i, REP)
        return remote(
            cot_in.at[to // 2], cot_r.at[peer, x], cot_ss.at[i], cot_rs.at[rep], to, exp
        )

    def mom_copy(i):
        to = lax.rem(chip + i, CHIPS)
        return remote(
            mom_in.at[to], mom_r.at[chip], mom_ss.at[i], mom_rs.at[chip], to * 2 + core, exp
        )

    tok_local = pltpu.make_async_copy(tok_in.at[exp], tok_r.at[x, exp], local_sem.at[0])
    cot_local = pltpu.make_async_copy(cot_in.at[chip], cot_r.at[peer, x], local_sem.at[1])
    mom_local = pltpu.make_async_copy(mom_in.at[chip], mom_r.at[chip], local_sem.at[2])

    tok_copy(0, 1).start()

    def start_tok(i, carry):
        tok_copy(i, 0).start()
        tok_copy(i, 1).start()
        return carry

    lax.fori_loop(1, EXP, start_tok, 0)

    def start_cot(i, carry):
        cot_copy(i).start()
        return carry

    lax.fori_loop(1, REP, start_cot, 0)

    def start_mom(i, carry):
        mom_copy(i).start()
        return carry

    lax.fori_loop(1, CHIPS, start_mom, 0)
    tok_local.start()
    cot_local.start()
    mom_local.start()

    out_row = lax.broadcasted_iota(jnp.int32, (SHARD, SHARD), 0)
    in_row = lax.broadcasted_iota(jnp.int32, (SHARD, SHARD), 1)
    wanted = (
        lax.rem(out_row // SLOTS, EXP) * (EXPERTS_HERE * SLOTS)
        + (out_row // TOKENS) * SLOTS
        + lax.rem(out_row, SLOTS)
    )
    order = jnp.where(in_row == wanted, 1.0, 0.0).astype(bf16)

    def wait_tok(i, carry):
        source = lax.rem(exp + i, EXP)
        remote(
            tok_in.at[0], tok_r.at[x, source], tok_ss.at[0, i], tok_rs.at[x, source], rep, source
        ).wait_recv()
        return carry

    lax.fori_loop(1, EXP, wait_tok, 0)

    def wait_tok_x(i, carry):
        source = lax.rem(exp + i, EXP)
        remote(
            tok_in.at[0],
            tok_r.at[1 - x, source],
            tok_ss.at[1, i],
            tok_rs.at[1 - x, source],
            rep_x,
            source,
        ).wait_recv()
        return carry

    lax.fori_loop(0, EXP, wait_tok_x, 0)
    tok_local.wait()

    for side in range(2):
        rows = tok_r[side].reshape(EXP * EXPERTS_HERE * SLOTS, WIDTH)
        for piece in range(REP):
            part = dot32(order, rows[:, piece * SHARD : (piece + 1) * SHARD]).astype(bf16)
            for expert in range(EXPERTS_HERE):
                t2_s[
                    expert * 2 + piece % 2,
                    side * TOKENS : (side + 1) * TOKENS,
                    (piece // 2) * SHARD : (piece // 2 + 1) * SHARD,
                ] = part[expert * TOKENS : (expert + 1) * TOKENS]

    def t2_copy(i):
        to = lax.rem(peer + i, CHIPS)
        return remote(
            t2_s.at[to],
            t2_r.at[peer],
            t2_ss.at[i],
            t2_rs.at[peer],
            (to // 2) * 4 + x * 2 + lax.rem(to, 2),
            exp,
        )

    def start_t2(i, carry):
        t2_copy(i).start()
        return carry

    lax.fori_loop(1, CHIPS, start_t2, 0)
    t2_local = pltpu.make_async_copy(t2_s.at[peer], t2_r.at[peer], local_sem.at[3])
    t2_local.start()

    def wait_cot(i, carry):
        source = lax.rem(rep + i, REP)
        from_peer = (source // 4) * 2 + lax.rem(source, 2)
        from_x = lax.rem(source // 2, 2)
        remote(
            cot_in.at[0],
            cot_r.at[from_peer, from_x],
            cot_ss.at[i],
            cot_rs.at[source],
            source,
            exp,
        ).wait_recv()
        return carry

    lax.fori_loop(1, REP, wait_cot, 0)
    cot_local.wait()

    def wait_mom(i, carry):
        source = lax.rem(chip + i, CHIPS)
        remote(
            mom_in.at[0],
            mom_r.at[source],
            mom_ss.at[i],
            mom_rs.at[source],
            source * 2 + core,
            exp,
        ).wait_recv()
        return carry

    lax.fori_loop(1, CHIPS, wait_mom, 0)
    mom_local.wait()

    def wait_t2(i, carry):
        source = lax.rem(peer + i, CHIPS)
        remote(
            t2_s.at[0],
            t2_r.at[source],
            t2_ss.at[i],
            t2_rs.at[source],
            (source // 2) * 4 + x * 2 + lax.rem(source, 2),
            exp,
        ).wait_recv()
        return carry

    lax.fori_loop(1, CHIPS, wait_t2, 0)
    t2_local.wait()

    def new_copy(i):
        to = lax.rem(chip + i, CHIPS)
        return remote(
            new_s.at[to], new_out.at[chip], new_ss.at[i], new_rs.at[chip], to * 2 + core, exp
        )

    sq_s[...] = jnp.zeros_like(sq_s)
    cots = cot_r[...].reshape(REP * TOKENS, HIDDEN)

    def gradient(i):
        at = lax.rem(chip + i, CHIPS)
        columns = pl.ds(pl.multiple_of(at * SHARD, SHARD), SHARD)
        feats = t2_r[:, :, columns].reshape(REP * TOKENS, SHARD)
        grad = dot_rows(feats, cots)
        mom = decay_rate * mom_r[at].astype(f32) + grad
        new_s[at] = mom.astype(bf16)
        nest = (grad + decay_rate * mom).astype(bf16)
        nest_s[at] = nest
        wide = nest.astype(f32)
        squares = jnp.sum((wide * wide).reshape(SHARD // 8, 8, HIDDEN // 128, 128), axis=(0, 2))
        sq_s[...] += squares

    def gradient_send(i, carry):
        gradient(i)
        new_copy(i).start()
        return carry

    lax.fori_loop(1, CHIPS, gradient_send, 0)
    gradient(0)
    new_local = pltpu.make_async_copy(new_s.at[chip], new_out.at[chip], local_sem.at[4])
    new_local.start()

    def gram_tile(j, carry):
        columns = pl.ds(pl.multiple_of(j * TILE, TILE), TILE)
        values = nest_s[...].reshape(CHIPS * SHARD, HIDDEN)
        tile = dot_rows(values, nest_s[:, :, columns].reshape(CHIPS * SHARD, TILE))
        gram_f[:, columns] = tile
        gram_s[:, columns] = tile.astype(bf16)
        return carry

    lax.fori_loop(0, HIDDEN // TILE, gram_tile, 0)
    swap_gram = remote(gram_s, gram_r, pair_ss.at[0], pair_rs.at[0], rep_core, exp)
    swap_sq = remote(sq_s, sq_r, pair_ss.at[1], pair_rs.at[1], rep_core, exp)
    swap_gram.start()
    swap_sq.start()
    swap_sq.wait()
    swap_gram.wait()

    total = jnp.sum(jnp.sum(sq_s[...] + sq_r[...], axis=0, keepdims=True), axis=1, keepdims=True)
    inverse = 1.0 / (jnp.sqrt(total) + norm_eps)
    g0[...] = ((gram_f[...] + gram_r[...].astype(f32)) * inverse * inverse).astype(bf16)

    def tiles(body):
        def one(j, carry):
            body(pl.ds(pl.multiple_of(j * TILE, TILE), TILE))
            return carry

        lax.fori_loop(0, HIDDEN // TILE, one, 0)

    def bend0_tile(at):
        bend0[:, at] = (
            coef_b * g0[:, at].astype(f32) + coef_c * dot32(g0[...], g0[:, at])
        ).astype(bf16)

    def step_tile(at):
        step[:, at] = (
            coef_a * g0[:, at].astype(f32) + dot32(g0[...], bend0[:, at])
        ).astype(bf16)

    def g1_tile(at):
        g1[:, at] = (
            coef_a * step[:, at].astype(f32) + dot32(bend0[...], step[:, at])
        ).astype(bf16)

    def bend1_tile(at):
        bend1[:, at] = (
            coef_b * g1[:, at].astype(f32) + coef_c * dot32(g1[...], g1[:, at])
        ).astype(bf16)

    def both_tile(at):
        both[:, at] = (
            coef_a * (bend0[:, at].astype(f32) + bend1[:, at].astype(f32))
            + dot32(bend0[...], bend1[:, at])
        ).astype(bf16)

    for body in (bend0_tile, step_tile, g1_tile, bend1_tile, both_tile):
        tiles(body)

    scale = math.sqrt(WIDTH) * inverse

    def upd_copy(i):
        to = lax.rem(chip + i, CHIPS)
        return remote(
            upd_s.at[to], upd_out.at[chip], upd_ss.at[i], upd_rs.at[chip], to * 2 + core, exp
        )

    def turn(i):
        at = lax.rem(chip + i, CHIPS)
        rows = nest_s[at]
        turned = coef_a * coef_a * rows.astype(f32) + dot32(rows, both[...])
        upd_s[at] = (turned * scale).astype(bf16)

    def turn_send(i, carry):
        turn(i)
        upd_copy(i).start()
        return carry

    lax.fori_loop(1, CHIPS, turn_send, 0)
    turn(0)
    upd_local = pltpu.make_async_copy(upd_s.at[chip], upd_out.at[chip], local_sem.at[5])
    upd_local.start()

    tok_copy(0, 1).wait_send()

    def finish_tok(i, carry):
        tok_copy(i, 0).wait_send()
        tok_copy(i, 1).wait_send()
        cot_copy(i).wait_send()
        return carry

    lax.fori_loop(1, EXP, finish_tok, 0)

    def finish(i, carry):
        mom_copy(i).wait_send()
        t2_copy(i).wait_send()
        new_copy(i).wait_send()
        upd_copy(i).wait_send()
        source = lax.rem(chip + i, CHIPS)
        remote(
            new_s.at[0],
            new_out.at[source],
            new_ss.at[i],
            new_rs.at[source],
            source * 2 + core,
            exp,
        ).wait_recv()
        remote(
            upd_s.at[0],
            upd_out.at[source],
            upd_ss.at[i],
            upd_rs.at[source],
            source * 2 + core,
            exp,
        ).wait_recv()
        return carry

    lax.fori_loop(1, CHIPS, finish, 0)
    new_local.wait()
    upd_local.wait()


def on_device(acts, cotangent, counts, momentum):
    slot_count = acts.shape[3]
    slot_index = lax.broadcasted_iota(jnp.int32, (1, 1, 1, slot_count, 1), 3)
    live_rows = slot_index < counts[:, :, :, None, None]
    live = jnp.where(live_rows, acts, jnp.zeros_like(acts))
    tok = live.reshape(EXP, EXPERTS_HERE * SLOTS, WIDTH)
    cot = cotangent.reshape(CHIPS, TOKENS, HIDDEN)
    mom = momentum.transpose(1, 2, 0, 3).reshape(CHIPS, SHARD, HIDDEN)
    vmem = pltpu.VMEM
    dma = pltpu.SemaphoreType.DMA
    square = (HIDDEN, HIDDEN)
    rows = (CHIPS, SHARD, HIDDEN)
    new_rows, upd_rows = pl.pallas_call(
        kernel,
        out_shape=[jax.ShapeDtypeStruct(rows, bf16)] * 2,
        in_specs=[pl.BlockSpec(memory_space=pl.ANY)] * 3,
        out_specs=[pl.BlockSpec(memory_space=pl.ANY)] * 2,
        scratch_shapes=[
            vmem((2, EXP, EXPERTS_HERE * SLOTS, WIDTH), bf16),
            vmem((CHIPS, 2 * TOKENS, HALF), bf16),
            vmem((CHIPS, 2 * TOKENS, HALF), bf16),
            vmem((CHIPS, 2, TOKENS, HIDDEN), bf16),
            vmem(rows, bf16),
            vmem(rows, bf16),
            vmem(rows, bf16),
            vmem(rows, bf16),
            vmem(square, bf16),
            vmem(square, bf16),
            vmem(square, f32),
            vmem((8, 128), f32),
            vmem((8, 128), f32),
            vmem(square, bf16),
            vmem(square, bf16),
            vmem(square, bf16),
            vmem(square, bf16),
            vmem(square, bf16),
            vmem(square, bf16),
            dma((2, EXP)),
            dma((2, EXP)),
            dma((REP,)),
            dma((REP,)),
            dma((CHIPS,)),
            dma((CHIPS,)),
            dma((CHIPS,)),
            dma((CHIPS,)),
            dma((CHIPS,)),
            dma((CHIPS,)),
            dma((CHIPS,)),
            dma((CHIPS,)),
            dma((2,)),
            dma((2,)),
            dma((6,)),
        ],
        compiler_params=pltpu.CompilerParams(
            collective_id=0, has_side_effects=True, vmem_limit_bytes=48 << 20
        ),
        name="muon_owner",
    )(tok, cot, mom)
    shape = (EXPERTS_HERE, 2, SHARD, HIDDEN)
    new_momentum = new_rows.reshape(shape).transpose(2, 0, 1, 3)
    update = upd_rows.reshape(shape).transpose(2, 0, 1, 3)
    return (new_momentum, update)


def solution(mesh):
    in_specs = (
        P("rep", "exp", None, None, None),
        P("rep", "exp", None, None, None),
        P("rep", "exp", None),
        P("rep", "exp", None, None),
    )
    out_specs = (P("rep", "exp", None, None), P("rep", "exp", None, None))
    return jax.shard_map(
        on_device, mesh=mesh, in_specs=in_specs, out_specs=out_specs, check_vma=False
    )
```

```python
import functools
import math

import jax
import jax.numpy as jnp
from jax import lax
from jax.experimental import pallas as pl
from jax.experimental.pallas import tpu as pltpu
from jax.sharding import PartitionSpec as P

coef_a = 3.4445
coef_b = -4.775
coef_c = 2.0315
decay_rate = 0.95
norm_eps = 1e-07

REP = 16
EXP = 16
CHIPS = 8
YS = 4
EXPERTS_HERE = 4
SIDES = 2
SIDE_EXPERTS = EXPERTS_HERE // SIDES
SLOTS = 2
SIDE_ROWS = SIDE_EXPERTS * SLOTS
WIDTH = 2048
HALF = WIDTH // 2
SHARD = 128
HIDDEN = 768
TOKENS = 32
TILE = 256

MESH = pl.DeviceIdType.MESH
f32 = jnp.float32
bf16 = jnp.bfloat16


def remote(src, dst, send_sem, recv_sem, rep, exp):
    return pltpu.make_async_remote_copy(
        src_ref=src,
        dst_ref=dst,
        send_sem=send_sem,
        recv_sem=recv_sem,
        device_id=(rep, exp),
        device_id_type=MESH,
    )


def dot32(left, right):
    return jnp.dot(left, right, preferred_element_type=f32)


def dot_rows(left, right):
    return lax.dot_general(left, right, (((0,), (0,)), ((), ())), preferred_element_type=f32)


def kernel(
    counts,
    acts_in,
    cot_in,
    mom_in,
    new_out,
    upd_out,
    tok_in,
    tok_r,
    t2_s,
    t2_r,
    cot_r,
    mom_r,
    new_s,
    nest_s,
    upd_s,
    gram_s,
    gram_r,
    gram_f,
    sq_s,
    sq_r,
    g0,
    bend0,
    step,
    g1,
    bend1,
    both,
    tok_ss,
    tok_rs,
    cot_ss,
    cot_rs,
    fwd_ss,
    mom_ss,
    mom_rs,
    t2_ss,
    t2_rs,
    new_ss,
    new_rs,
    upd_ss,
    upd_rs,
    pair_ss,
    pair_rs,
    local_sem,
):
    rep = lax.axis_index("rep")
    exp = lax.axis_index("exp")
    chip = rep // 2
    core = lax.rem(rep, 2)
    y = rep // 4
    x = lax.rem(chip, 2)
    peer = y * 2 + core
    rep_x = y * 4 + (1 - x) * 2 + core
    rep_core = chip * 2 + (1 - core)
    mine = 4 * x + y

    def matrix(of_chip):
        return 4 * lax.rem(of_chip, 2) + of_chip // 2

    def signal(to_rep, to_exp):
        pl.semaphore_signal(
            pltpu.get_barrier_semaphore(), inc=1, device_id=(to_rep, to_exp), device_id_type=MESH
        )

    def greet(i, carry):
        signal(rep, lax.rem(exp + i, EXP))
        signal(lax.rem(rep + i, REP), exp)
        signal(rep_x, lax.rem(exp + i, EXP))
        return carry

    lax.fori_loop(1, 16, greet, 0)

    row = lax.broadcasted_iota(jnp.int32, (SIDE_ROWS, WIDTH), 0)

    def mask(i, carry):
        group = i // SIDES
        side = lax.rem(i, SIDES)
        at = i * SIDE_EXPERTS
        count = jnp.where(row < SLOTS, counts[at], counts[at + 1])
        values = acts_in[group, side].astype(f32)
        tok_in[group, side] = jnp.where(lax.rem(row, SLOTS) < count, values, 0.0).astype(bf16)
        return carry

    lax.fori_loop(0, EXP * SIDES, mask, 0)
    pl.semaphore_wait(pltpu.get_barrier_semaphore(), 45)

    def tok_copy(i, other):
        to = lax.rem(exp + i, EXP)
        return remote(
            tok_in.at[to, 1 - x if other else x],
            tok_r.at[x, exp],
            tok_ss.at[other, i],
            tok_rs.at[x, exp],
            rep_x if other else rep,
            to,
        )

    def cot_copy(i):
        to = lax.rem(chip + i, CHIPS)
        return remote(
            cot_in.at[matrix(to)],
            cot_r.at[peer, x],
            cot_ss.at[i],
            cot_rs.at[peer, x],
            to * 2 + core,
            exp,
        )

    def mom_copy(i):
        to = lax.rem(chip + i, CHIPS)
        return remote(
            mom_in.at[matrix(to)],
            mom_r.at[chip],
            mom_ss.at[i],
            mom_rs.at[chip],
            to * 2 + core,
            exp,
        )

    tok_local = pltpu.make_async_copy(tok_in.at[exp, x], tok_r.at[x, exp], local_sem.at[0])
    cot_local = pltpu.make_async_copy(cot_in.at[mine], cot_r.at[peer, x], local_sem.at[1])
    mom_local = pltpu.make_async_copy(mom_in.at[mine], mom_r.at[chip], local_sem.at[2])

    tok_copy(0, 1).start()

    def start_tok(i, carry):
        tok_copy(i, 0).start()
        tok_copy(i, 1).start()
        return carry

    lax.fori_loop(1, EXP, start_tok, 0)

    def start_cot(i, carry):
        cot_copy(i).start()
        return carry

    lax.fori_loop(1, CHIPS, start_cot, 0)

    def start_mom(i, carry):
        mom_copy(i).start()
        return carry

    lax.fori_loop(1, CHIPS, start_mom, 0)
    tok_local.start()
    cot_local.start()
    mom_local.start()

    out_row = lax.broadcasted_iota(jnp.int32, (SHARD, SHARD), 0)
    in_row = lax.broadcasted_iota(jnp.int32, (SHARD, SHARD), 1)
    wanted = (
        lax.rem(out_row // SLOTS, SIDES * EXP) * SIDE_ROWS
        + (out_row // (SIDES * TOKENS)) * SLOTS
        + lax.rem(out_row, SLOTS)
    )
    order = jnp.where(in_row == wanted, 1.0, 0.0).astype(bf16)

    def wait_tok(i, carry):
        source = lax.rem(exp + i, EXP)
        remote(
            tok_in.at[0, 0], tok_r.at[x, source], tok_ss.at[0, i], tok_rs.at[x, source], rep, source
        ).wait_recv()
        return carry

    lax.fori_loop(1, EXP, wait_tok, 0)

    def wait_tok_x(i, carry):
        source = lax.rem(exp + i, EXP)
        remote(
            tok_in.at[0, 0],
            tok_r.at[1 - x, source],
            tok_ss.at[1, i],
            tok_rs.at[1 - x, source],
            rep_x,
            source,
        ).wait_recv()
        return carry

    lax.fori_loop(0, EXP, wait_tok_x, 0)
    tok_local.wait()

    rows = tok_r[...].reshape(SIDES * EXP * SIDE_ROWS, WIDTH)
    for piece in range(REP):
        part = dot32(order, rows[:, piece * SHARD : (piece + 1) * SHARD]).astype(bf16)
        for expert in range(SIDE_EXPERTS):
            t2_s[expert, piece % 2, :, (piece // 2) * SHARD : (piece // 2 + 1) * SHARD] = part[
                expert * SIDES * TOKENS : (expert + 1) * SIDES * TOKENS
            ]

    def t2_copy(i):
        to = lax.rem(peer + i, CHIPS)
        return remote(
            t2_s.at[to // 4, lax.rem(to, 2)],
            t2_r.at[peer],
            t2_ss.at[i],
            t2_rs.at[peer],
            (to // 2) * 4 + x * 2 + lax.rem(to, 2),
            exp,
        )

    def start_t2(i, carry):
        t2_copy(i).start()
        return carry

    lax.fori_loop(1, CHIPS, start_t2, 0)
    t2_local = pltpu.make_async_copy(t2_s.at[y // 2, core], t2_r.at[peer], local_sem.at[3])
    t2_local.start()

    def forward(of_chip):
        at = (of_chip // 2) * 2 + core
        side = lax.rem(of_chip, 2)
        return remote(
            cot_r.at[at, side],
            cot_r.at[at, side],
            fwd_ss.at[of_chip],
            cot_rs.at[at, side],
            rep_core,
            exp,
        )

    def wait_cot(i, carry):
        source = lax.rem(chip + i, CHIPS)
        at = (source // 2) * 2 + core
        side = lax.rem(source, 2)
        remote(
            cot_in.at[0],
            cot_r.at[at, side],
            cot_ss.at[i],
            cot_rs.at[at, side],
            source * 2 + core,
            exp,
        ).wait_recv()
        forward(source).start()
        return carry

    cot_local.wait()
    forward(chip).start()
    lax.fori_loop(1, CHIPS, wait_cot, 0)

    def wait_forward(i, carry):
        at = (i // 2) * 2 + 1 - core
        side = lax.rem(i, 2)
        remote(
            cot_r.at[at, side],
            cot_r.at[at, side],
            fwd_ss.at[i],
            cot_rs.at[at, side],
            rep_core,
            exp,
        ).wait_recv()
        return carry

    lax.fori_loop(0, CHIPS, wait_forward, 0)

    def wait_mom(source):
        remote(
            mom_in.at[0],
            mom_r.at[source],
            mom_ss.at[0],
            mom_rs.at[source],
            source * 2 + core,
            exp,
        ).wait_recv()

    def wait_t2(i, carry):
        source = lax.rem(peer + i, CHIPS)
        remote(
            t2_s.at[0],
            t2_r.at[source],
            t2_ss.at[i],
            t2_rs.at[source],
            (source // 2) * 4 + x * 2 + lax.rem(source, 2),
            exp,
        ).wait_recv()
        return carry

    lax.fori_loop(1, CHIPS, wait_t2, 0)
    t2_local.wait()

    def new_copy(i):
        to = lax.rem(chip + i, CHIPS)
        return remote(
            new_s.at[to], new_out.at[mine], new_ss.at[i], new_rs.at[chip], to * 2 + core, exp
        )

    sq_s[...] = jnp.zeros_like(sq_s)
    cots = cot_r[...].reshape(REP * TOKENS, HIDDEN)

    def gradient(i):
        at = lax.rem(chip + i, CHIPS)
        columns = pl.ds(pl.multiple_of(at * SHARD, SHARD), SHARD)
        feats = t2_r[:, :, columns].reshape(REP * TOKENS, SHARD)
        grad = dot_rows(feats, cots)
        mom = decay_rate * mom_r[at].astype(f32) + grad
        new_s[at] = mom.astype(bf16)
        nest = (grad + decay_rate * mom).astype(bf16)
        nest_s[at] = nest
        wide = nest.astype(f32)
        squares = jnp.sum((wide * wide).reshape(SHARD // 8, 8, HIDDEN // 128, 128), axis=(0, 2))
        sq_s[...] += squares

    def gradient_send(i, carry):
        wait_mom(lax.rem(chip + i, CHIPS))
        gradient(i)
        new_copy(i).start()
        return carry

    lax.fori_loop(1, CHIPS, gradient_send, 0)
    mom_local.wait()
    gradient(0)
    new_local = pltpu.make_async_copy(new_s.at[chip], new_out.at[mine], local_sem.at[4])
    new_local.start()

    def gram_tile(j, carry):
        columns = pl.ds(pl.multiple_of(j * TILE, TILE), TILE)
        values = nest_s[...].reshape(CHIPS * SHARD, HIDDEN)
        tile = dot_rows(values, nest_s[:, :, columns].reshape(CHIPS * SHARD, TILE))
        gram_f[:, columns] = tile
        gram_s[:, columns] = tile.astype(bf16)
        return carry

    lax.fori_loop(0, HIDDEN // TILE, gram_tile, 0)
    swap_gram = remote(gram_s, gram_r, pair_ss.at[0], pair_rs.at[0], rep_core, exp)
    swap_sq = remote(sq_s, sq_r, pair_ss.at[1], pair_rs.at[1], rep_core, exp)
    swap_gram.start()
    swap_sq.start()
    swap_sq.wait()
    swap_gram.wait()

    total = jnp.sum(jnp.sum(sq_s[...] + sq_r[...], axis=0, keepdims=True), axis=1, keepdims=True)
    inverse = 1.0 / (jnp.sqrt(total) + norm_eps)
    g0[...] = ((gram_f[...] + gram_r[...].astype(f32)) * inverse * inverse).astype(bf16)

    def tiles(body):
        def one(j, carry):
            body(pl.ds(pl.multiple_of(j * TILE, TILE), TILE))
            return carry

        lax.fori_loop(0, HIDDEN // TILE, one, 0)

    def bend0_tile(at):
        bend0[:, at] = (
            coef_b * g0[:, at].astype(f32) + coef_c * dot32(g0[...], g0[:, at])
        ).astype(bf16)

    def step_tile(at):
        step[:, at] = (
            coef_a * g0[:, at].astype(f32) + dot32(g0[...], bend0[:, at])
        ).astype(bf16)

    def g1_tile(at):
        g1[:, at] = (
            coef_a * step[:, at].astype(f32) + dot32(bend0[...], step[:, at])
        ).astype(bf16)

    def bend1_tile(at):
        bend1[:, at] = (
            coef_b * g1[:, at].astype(f32) + coef_c * dot32(g1[...], g1[:, at])
        ).astype(bf16)

    def both_tile(at):
        both[:, at] = (
            coef_a * (bend0[:, at].astype(f32) + bend1[:, at].astype(f32))
            + dot32(bend0[...], bend1[:, at])
        ).astype(bf16)

    for body in (bend0_tile, step_tile, g1_tile, bend1_tile, both_tile):
        tiles(body)

    scale = math.sqrt(WIDTH) * inverse

    def upd_copy(i):
        to = lax.rem(chip + i, CHIPS)
        return remote(
            upd_s.at[to], upd_out.at[mine], upd_ss.at[i], upd_rs.at[chip], to * 2 + core, exp
        )

    def turn(i):
        at = lax.rem(chip + i, CHIPS)
        rows = nest_s[at]
        turned = coef_a * coef_a * rows.astype(f32) + dot32(rows, both[...])
        upd_s[at] = (turned * scale).astype(bf16)

    def turn_send(i, carry):
        turn(i)
        upd_copy(i).start()
        return carry

    lax.fori_loop(1, CHIPS, turn_send, 0)
    turn(0)
    upd_local = pltpu.make_async_copy(upd_s.at[chip], upd_out.at[mine], local_sem.at[5])
    upd_local.start()

    tok_copy(0, 1).wait_send()

    def finish_tok(i, carry):
        tok_copy(i, 0).wait_send()
        tok_copy(i, 1).wait_send()
        return carry

    lax.fori_loop(1, EXP, finish_tok, 0)

    forward(chip).wait_send()

    def finish(i, carry):
        cot_copy(i).wait_send()
        forward(lax.rem(chip + i, CHIPS)).wait_send()
        mom_copy(i).wait_send()
        t2_copy(i).wait_send()
        new_copy(i).wait_send()
        upd_copy(i).wait_send()
        source = lax.rem(chip + i, CHIPS)
        remote(
            new_s.at[0],
            new_out.at[matrix(source)],
            new_ss.at[i],
            new_rs.at[source],
            source * 2 + core,
            exp,
        ).wait_recv()
        remote(
            upd_s.at[0],
            upd_out.at[matrix(source)],
            upd_ss.at[i],
            upd_rs.at[source],
            source * 2 + core,
            exp,
        ).wait_recv()
        return carry

    lax.fori_loop(1, CHIPS, finish, 0)
    new_local.wait()
    upd_local.wait()


def on_device(acts, cotangent, counts, momentum):
    live = counts.reshape(EXP * EXPERTS_HERE)
    tok = acts.reshape(EXP, SIDES, SIDE_ROWS, WIDTH)
    cot = cotangent.reshape(CHIPS, TOKENS, HIDDEN)
    mom = momentum.transpose(1, 2, 0, 3).reshape(CHIPS, SHARD, HIDDEN)
    vmem = pltpu.VMEM
    dma = pltpu.SemaphoreType.DMA
    square = (HIDDEN, HIDDEN)
    rows = (CHIPS, SHARD, HIDDEN)
    new_rows, upd_rows = pl.pallas_call(
        kernel,
        out_shape=[jax.ShapeDtypeStruct(rows, bf16)] * 2,
        in_specs=[
            pl.BlockSpec(memory_space=pltpu.SMEM),
            pl.BlockSpec(memory_space=pltpu.VMEM),
            pl.BlockSpec(memory_space=pl.ANY),
            pl.BlockSpec(memory_space=pl.ANY),
        ],
        out_specs=[pl.BlockSpec(memory_space=pl.ANY)] * 2,
        scratch_shapes=[
            vmem((EXP, SIDES, SIDE_ROWS, WIDTH), bf16),
            vmem((SIDES, EXP, SIDE_ROWS, WIDTH), bf16),
            vmem((SIDE_EXPERTS, 2, SIDES * TOKENS, HALF), bf16),
            vmem((CHIPS, 2 * TOKENS, HALF), bf16),
            vmem((CHIPS, 2, TOKENS, HIDDEN), bf16),
            vmem(rows, bf16),
            vmem(rows, bf16),
            vmem(rows, bf16),
            vmem(rows, bf16),
            vmem(square, bf16),
            vmem(square, bf16),
            vmem(square, f32),
            vmem((8, 128), f32),
            vmem((8, 128), f32),
            vmem(square, bf16),
            vmem(square, bf16),
            vmem(square, bf16),
            vmem(square, bf16),
            vmem(square, bf16),
            vmem(square, bf16),
            dma((2, EXP)),
            dma((2, EXP)),
            dma((CHIPS,)),
            dma((CHIPS, SIDES)),
            dma((CHIPS,)),
            dma((CHIPS,)),
            dma((CHIPS,)),
            dma((CHIPS,)),
            dma((CHIPS,)),
            dma((CHIPS,)),
            dma((CHIPS,)),
            dma((CHIPS,)),
            dma((CHIPS,)),
            dma((2,)),
            dma((2,)),
            dma((6,)),
        ],
        compiler_params=pltpu.CompilerParams(
            collective_id=0, has_side_effects=True, vmem_limit_bytes=48 << 20
        ),
        name="muon_owner",
    )(live, tok, cot, mom)
    shape = (EXPERTS_HERE, 2, SHARD, HIDDEN)
    new_momentum = new_rows.reshape(shape).transpose(2, 0, 1, 3)
    update = upd_rows.reshape(shape).transpose(2, 0, 1, 3)
    return (new_momentum, update)


def solution(mesh):
    in_specs = (
        P("rep", "exp", None, None, None),
        P("rep", "exp", None, None, None),
        P("rep", "exp", None),
        P("rep", "exp", None, None),
    )
    out_specs = (P("rep", "exp", None, None), P("rep", "exp", None, None))
    return jax.shard_map(
        on_device, mesh=mesh, in_specs=in_specs, out_specs=out_specs, check_vma=False
    )
```

```python
import functools
import math

import jax
import jax.numpy as jnp
from jax import lax
from jax.experimental import pallas as pl
from jax.experimental.pallas import tpu as pltpu
from jax.sharding import PartitionSpec as P

coef_a = 3.4445
coef_b = -4.775
coef_c = 2.0315
decay_rate = 0.95
norm_eps = 1e-07

REP = 16
EXP = 16
CHIPS = 8
YS = 4
EXPERTS_HERE = 4
SIDES = 2
SIDE_EXPERTS = EXPERTS_HERE // SIDES
SLOTS = 2
SIDE_ROWS = SIDE_EXPERTS * SLOTS
WIDTH = 2048
HALF = WIDTH // 2
SHARD = 128
HIDDEN = 768
TOKENS = 32
TILE = 256

MESH = pl.DeviceIdType.MESH
f32 = jnp.float32
bf16 = jnp.bfloat16


def remote(src, dst, send_sem, recv_sem, rep, exp):
    return pltpu.make_async_remote_copy(
        src_ref=src,
        dst_ref=dst,
        send_sem=send_sem,
        recv_sem=recv_sem,
        device_id=(rep, exp),
        device_id_type=MESH,
    )


def dot32(left, right):
    return jnp.dot(left, right, preferred_element_type=f32)


def dot_rows(left, right):
    return lax.dot_general(left, right, (((0,), (0,)), ((), ())), preferred_element_type=f32)


def kernel(
    counts,
    acts_hbm,
    cot_in,
    mom_hbm,
    new_hbm,
    upd_hbm,
    acts_in,
    mom_raw,
    mom_in,
    new_out,
    upd_out,
    new_mix,
    upd_mix,
    tok_in,
    tok_r,
    t2_s,
    t2_r,
    cot_r,
    mom_r,
    new_s,
    nest_s,
    upd_s,
    gram_s,
    gram_r,
    gram_f,
    sq_s,
    sq_r,
    g0,
    bend0,
    step,
    g1,
    bend1,
    both,
    tok_ss,
    tok_rs,
    cot_ss,
    cot_rs,
    fwd_ss,
    mom_ss,
    mom_rs,
    t2_ss,
    t2_rs,
    new_ss,
    new_rs,
    upd_ss,
    upd_rs,
    pair_ss,
    pair_rs,
    local_sem,
):
    rep = lax.axis_index("rep")
    exp = lax.axis_index("exp")
    chip = rep // 2
    core = lax.rem(rep, 2)
    y = rep // 4
    x = lax.rem(chip, 2)
    peer = y * 2 + core
    rep_x = y * 4 + (1 - x) * 2 + core
    rep_core = chip * 2 + (1 - core)
    mine = 4 * x + y

    def matrix(of_chip):
        return 4 * lax.rem(of_chip, 2) + of_chip // 2

    def signal(to_rep, to_exp):
        pl.semaphore_signal(
            pltpu.get_barrier_semaphore(), inc=1, device_id=(to_rep, to_exp), device_id_type=MESH
        )

    def greet(i, carry):
        signal(rep, lax.rem(exp + i, EXP))
        signal(lax.rem(rep + i, REP), exp)
        signal(rep_x, lax.rem(exp + i, EXP))
        return carry

    lax.fori_loop(1, 16, greet, 0)
    acts_load = pltpu.make_async_copy(acts_hbm, acts_in, local_sem.at[6])
    mom_load = pltpu.make_async_copy(mom_hbm, mom_raw, local_sem.at[7])
    acts_load.start()
    mom_load.start()

    row = lax.broadcasted_iota(jnp.int32, (SIDE_ROWS, WIDTH), 0)

    def mask(i, carry):
        group = i // SIDES
        side = lax.rem(i, SIDES)
        at = i * SIDE_EXPERTS
        count = jnp.where(row < SLOTS, counts[at], counts[at + 1])
        values = acts_in[pl.ds(at, SIDE_EXPERTS)].astype(f32).reshape(SIDE_ROWS, WIDTH)
        tok_in[group, side] = jnp.where(lax.rem(row, SLOTS) < count, values, 0.0).astype(bf16)
        return carry

    acts_load.wait()
    lax.fori_loop(0, EXP * SIDES, mask, 0)
    pl.semaphore_wait(pltpu.get_barrier_semaphore(), 45)

    def tok_copy(i, other):
        to = lax.rem(exp + i, EXP)
        return remote(
            tok_in.at[to, 1 - x if other else x],
            tok_r.at[x, exp],
            tok_ss.at[other, i],
            tok_rs.at[x, exp],
            rep_x if other else rep,
            to,
        )

    def cot_copy(i):
        to = lax.rem(chip + i, CHIPS)
        return remote(
            cot_in.at[matrix(to)],
            cot_r.at[peer, x],
            cot_ss.at[i],
            cot_rs.at[peer, x],
            to * 2 + core,
            exp,
        )

    def mom_copy(i):
        to = lax.rem(chip + i, CHIPS)
        return remote(
            mom_in.at[matrix(to)],
            mom_r.at[chip],
            mom_ss.at[i],
            mom_rs.at[chip],
            to * 2 + core,
            exp,
        )

    tok_local = pltpu.make_async_copy(tok_in.at[exp, x], tok_r.at[x, exp], local_sem.at[0])
    cot_local = pltpu.make_async_copy(cot_in.at[mine], cot_r.at[peer, x], local_sem.at[1])
    mom_local = pltpu.make_async_copy(mom_in.at[mine], mom_r.at[chip], local_sem.at[2])

    tok_copy(0, 1).start()

    def start_tok(i, carry):
        tok_copy(i, 0).start()
        tok_copy(i, 1).start()
        return carry

    lax.fori_loop(1, EXP, start_tok, 0)

    def start_cot(i, carry):
        cot_copy(i).start()
        return carry

    lax.fori_loop(1, CHIPS, start_cot, 0)

    mom_load.wait()
    for expert in range(EXPERTS_HERE):
        mom_in[2 * expert : 2 * expert + 2] = jnp.swapaxes(mom_raw[:, expert], 0, 1)

    def start_mom(i, carry):
        mom_copy(i).start()
        return carry

    lax.fori_loop(1, CHIPS, start_mom, 0)
    tok_local.start()
    cot_local.start()
    mom_local.start()

    out_row = lax.broadcasted_iota(jnp.int32, (SHARD, SHARD), 0)
    in_row = lax.broadcasted_iota(jnp.int32, (SHARD, SHARD), 1)
    wanted = (
        lax.rem(out_row // SLOTS, SIDES * EXP) * SIDE_ROWS
        + (out_row // (SIDES * TOKENS)) * SLOTS
        + lax.rem(out_row, SLOTS)
    )
    order = jnp.where(in_row == wanted, 1.0, 0.0).astype(bf16)

    def wait_tok(i, carry):
        source = lax.rem(exp + i, EXP)
        remote(
            tok_in.at[0, 0], tok_r.at[x, source], tok_ss.at[0, i], tok_rs.at[x, source], rep, source
        ).wait_recv()
        return carry

    lax.fori_loop(1, EXP, wait_tok, 0)

    def wait_tok_x(i, carry):
        source = lax.rem(exp + i, EXP)
        remote(
            tok_in.at[0, 0],
            tok_r.at[1 - x, source],
            tok_ss.at[1, i],
            tok_rs.at[1 - x, source],
            rep_x,
            source,
        ).wait_recv()
        return carry

    lax.fori_loop(0, EXP, wait_tok_x, 0)
    tok_local.wait()

    rows = tok_r[...].reshape(SIDES * EXP * SIDE_ROWS, WIDTH)
    for piece in range(REP):
        part = dot32(order, rows[:, piece * SHARD : (piece + 1) * SHARD]).astype(bf16)
        for expert in range(SIDE_EXPERTS):
            t2_s[expert, piece % 2, :, (piece // 2) * SHARD : (piece // 2 + 1) * SHARD] = part[
                expert * SIDES * TOKENS : (expert + 1) * SIDES * TOKENS
            ]

    def t2_copy(i):
        to = lax.rem(peer + i, CHIPS)
        return remote(
            t2_s.at[to // 4, lax.rem(to, 2)],
            t2_r.at[peer],
            t2_ss.at[i],
            t2_rs.at[peer],
            (to // 2) * 4 + x * 2 + lax.rem(to, 2),
            exp,
        )

    def start_t2(i, carry):
        t2_copy(i).start()
        return carry

    lax.fori_loop(1, CHIPS, start_t2, 0)
    t2_local = pltpu.make_async_copy(t2_s.at[y // 2, core], t2_r.at[peer], local_sem.at[3])
    t2_local.start()

    def forward(of_chip):
        at = (of_chip // 2) * 2 + core
        side = lax.rem(of_chip, 2)
        return remote(
            cot_r.at[at, side],
            cot_r.at[at, side],
            fwd_ss.at[of_chip],
            cot_rs.at[at, side],
            rep_core,
            exp,
        )

    def wait_cot(i, carry):
        source = lax.rem(chip + i, CHIPS)
        at = (source // 2) * 2 + core
        side = lax.rem(source, 2)
        remote(
            cot_in.at[0],
            cot_r.at[at, side],
            cot_ss.at[i],
            cot_rs.at[at, side],
            source * 2 + core,
            exp,
        ).wait_recv()
        forward(source).start()
        return carry

    cot_local.wait()
    forward(chip).start()
    lax.fori_loop(1, CHIPS, wait_cot, 0)

    def wait_forward(i, carry):
        at = (i // 2) * 2 + 1 - core
        side = lax.rem(i, 2)
        remote(
            cot_r.at[at, side],
            cot_r.at[at, side],
            fwd_ss.at[i],
            cot_rs.at[at, side],
            rep_core,
            exp,
        ).wait_recv()
        return carry

    lax.fori_loop(0, CHIPS, wait_forward, 0)

    def wait_mom(source):
        remote(
            mom_in.at[0],
            mom_r.at[source],
            mom_ss.at[0],
            mom_rs.at[source],
            source * 2 + core,
            exp,
        ).wait_recv()

    def wait_t2(i, carry):
        source = lax.rem(peer + i, CHIPS)
        remote(
            t2_s.at[0],
            t2_r.at[source],
            t2_ss.at[i],
            t2_rs.at[source],
            (source // 2) * 4 + x * 2 + lax.rem(source, 2),
            exp,
        ).wait_recv()
        return carry

    lax.fori_loop(1, CHIPS, wait_t2, 0)
    t2_local.wait()

    def new_copy(i):
        to = lax.rem(chip + i, CHIPS)
        return remote(
            new_s.at[to], new_out.at[mine], new_ss.at[i], new_rs.at[mine], to * 2 + core, exp
        )

    sq_s[...] = jnp.zeros_like(sq_s)
    cots = cot_r[...].reshape(REP * TOKENS, HIDDEN)

    def gradient(i):
        at = lax.rem(chip + i, CHIPS)
        columns = pl.ds(pl.multiple_of(at * SHARD, SHARD), SHARD)
        feats = t2_r[:, :, columns].reshape(REP * TOKENS, SHARD)
        grad = dot_rows(feats, cots)
        mom = decay_rate * mom_r[at].astype(f32) + grad
        new_s[at] = mom.astype(bf16)
        nest = (grad + decay_rate * mom).astype(bf16)
        nest_s[at] = nest
        wide = nest.astype(f32)
        squares = jnp.sum((wide * wide).reshape(SHARD // 8, 8, HIDDEN // 128, 128), axis=(0, 2))
        sq_s[...] += squares

    def gradient_send(i, carry):
        wait_mom(lax.rem(chip + i, CHIPS))
        gradient(i)
        new_copy(i).start()
        return carry

    lax.fori_loop(1, CHIPS, gradient_send, 0)
    mom_local.wait()
    gradient(0)
    new_local = pltpu.make_async_copy(new_s.at[chip], new_out.at[mine], local_sem.at[4])
    new_local.start()

    def gram_tile(j, carry):
        columns = pl.ds(pl.multiple_of(j * TILE, TILE), TILE)
        values = nest_s[...].reshape(CHIPS * SHARD, HIDDEN)
        tile = dot_rows(values, nest_s[:, :, columns].reshape(CHIPS * SHARD, TILE))
        gram_f[:, columns] = tile
        gram_s[:, columns] = tile.astype(bf16)
        return carry

    lax.fori_loop(0, HIDDEN // TILE, gram_tile, 0)
    swap_gram = remote(gram_s, gram_r, pair_ss.at[0], pair_rs.at[0], rep_core, exp)
    swap_sq = remote(sq_s, sq_r, pair_ss.at[1], pair_rs.at[1], rep_core, exp)
    swap_gram.start()
    swap_sq.start()
    swap_sq.wait()
    swap_gram.wait()

    total = jnp.sum(jnp.sum(sq_s[...] + sq_r[...], axis=0, keepdims=True), axis=1, keepdims=True)
    inverse = 1.0 / (jnp.sqrt(total) + norm_eps)
    g0[...] = ((gram_f[...] + gram_r[...].astype(f32)) * inverse * inverse).astype(bf16)

    def tiles(body):
        def one(j, carry):
            body(pl.ds(pl.multiple_of(j * TILE, TILE), TILE))
            return carry

        lax.fori_loop(0, HIDDEN // TILE, one, 0)

    def bend0_tile(at):
        bend0[:, at] = (
            coef_b * g0[:, at].astype(f32) + coef_c * dot32(g0[...], g0[:, at])
        ).astype(bf16)

    def step_tile(at):
        step[:, at] = (
            coef_a * g0[:, at].astype(f32) + dot32(g0[...], bend0[:, at])
        ).astype(bf16)

    def g1_tile(at):
        g1[:, at] = (
            coef_a * step[:, at].astype(f32) + dot32(bend0[...], step[:, at])
        ).astype(bf16)

    def bend1_tile(at):
        bend1[:, at] = (
            coef_b * g1[:, at].astype(f32) + coef_c * dot32(g1[...], g1[:, at])
        ).astype(bf16)

    def both_tile(at):
        both[:, at] = (
            coef_a * (bend0[:, at].astype(f32) + bend1[:, at].astype(f32))
            + dot32(bend0[...], bend1[:, at])
        ).astype(bf16)

    for body in (bend0_tile, step_tile, g1_tile, bend1_tile, both_tile):
        tiles(body)

    scale = math.sqrt(WIDTH) * inverse

    def upd_copy(i):
        to = lax.rem(chip + i, CHIPS)
        return remote(
            upd_s.at[to], upd_out.at[mine], upd_ss.at[i], upd_rs.at[mine], to * 2 + core, exp
        )

    def turn(i):
        at = lax.rem(chip + i, CHIPS)
        rows = nest_s[at]
        turned = coef_a * coef_a * rows.astype(f32) + dot32(rows, both[...])
        upd_s[at] = (turned * scale).astype(bf16)

    def turn_send(i, carry):
        turn(i)
        upd_copy(i).start()
        return carry

    lax.fori_loop(1, CHIPS, turn_send, 0)
    turn(0)
    upd_local = pltpu.make_async_copy(upd_s.at[chip], upd_out.at[mine], local_sem.at[5])
    upd_local.start()

    def wait_new(i, carry):
        source = lax.rem(chip + i, CHIPS)
        remote(
            new_s.at[0],
            new_out.at[matrix(source)],
            new_ss.at[i],
            new_rs.at[matrix(source)],
            source * 2 + core,
            exp,
        ).wait_recv()
        return carry

    lax.fori_loop(1, CHIPS, wait_new, 0)
    new_local.wait()

    mix = jnp.where(
        out_row == lax.rem(in_row, SHARD // 2) * 2 + in_row // (SHARD // 2), 1.0, 0.0
    ).astype(bf16)

    def interleave(source, target, expert):
        for part in range(2):
            half = slice(part * (SHARD // 2), (part + 1) * (SHARD // 2))
            pair = jnp.concatenate(
                [source[2 * expert, half], source[2 * expert + 1, half]], axis=0
            )
            target[half, expert] = (
                dot32(mix, pair).astype(bf16).reshape(SHARD // 2, 2, HIDDEN)
            )

    for expert in range(EXPERTS_HERE):
        interleave(new_out, new_mix, expert)
    new_store = pltpu.make_async_copy(new_mix, new_hbm, local_sem.at[8])
    new_store.start()

    tok_copy(0, 1).wait_send()

    def finish_tok(i, carry):
        tok_copy(i, 0).wait_send()
        tok_copy(i, 1).wait_send()
        return carry

    lax.fori_loop(1, EXP, finish_tok, 0)

    forward(chip).wait_send()

    def finish(i, carry):
        cot_copy(i).wait_send()
        forward(lax.rem(chip + i, CHIPS)).wait_send()
        mom_copy(i).wait_send()
        t2_copy(i).wait_send()
        new_copy(i).wait_send()
        return carry

    lax.fori_loop(1, CHIPS, finish, 0)
    upd_local.wait()

    def wait_upd(i, carry):
        source = lax.rem(chip + i, CHIPS)
        remote(
            upd_s.at[0],
            upd_out.at[matrix(source)],
            upd_ss.at[i],
            upd_rs.at[matrix(source)],
            source * 2 + core,
            exp,
        ).wait_recv()
        return carry

    lax.fori_loop(1, CHIPS, wait_upd, 0)
    for expert in range(EXPERTS_HERE):
        interleave(upd_out, upd_mix, expert)
    upd_store = pltpu.make_async_copy(upd_mix, upd_hbm, local_sem.at[9])
    upd_store.start()

    def finish_upd(i, carry):
        upd_copy(i).wait_send()
        return carry

    lax.fori_loop(1, CHIPS, finish_upd, 0)
    new_store.wait()
    upd_store.wait()


def on_device(acts, cotangent, counts, momentum):
    live = counts.reshape(EXP * EXPERTS_HERE)
    tok = acts.reshape(EXP * EXPERTS_HERE, SLOTS, WIDTH)
    cot = cotangent.reshape(CHIPS, TOKENS, HIDDEN)
    vmem = pltpu.VMEM
    dma = pltpu.SemaphoreType.DMA
    square = (HIDDEN, HIDDEN)
    rows = (CHIPS, SHARD, HIDDEN)
    mixed = (SHARD, EXPERTS_HERE, 2, HIDDEN)
    return pl.pallas_call(
        kernel,
        out_shape=(jax.ShapeDtypeStruct(mixed, bf16),) * 2,
        in_specs=[
            pl.BlockSpec(memory_space=pltpu.SMEM),
            pl.BlockSpec(memory_space=pl.ANY),
            pl.BlockSpec(memory_space=pl.ANY),
            pl.BlockSpec(memory_space=pl.ANY),
        ],
        out_specs=(pl.BlockSpec(memory_space=pl.ANY),) * 2,
        scratch_shapes=[
            vmem((EXP * EXPERTS_HERE, SLOTS, WIDTH), bf16),
            vmem(mixed, bf16),
            vmem(rows, bf16),
            vmem(rows, bf16),
            vmem(rows, bf16),
            vmem(mixed, bf16),
            vmem(mixed, bf16),
            vmem((EXP, SIDES, SIDE_ROWS, WIDTH), bf16),
            vmem((SIDES, EXP, SIDE_ROWS, WIDTH), bf16),
            vmem((SIDE_EXPERTS, 2, SIDES * TOKENS, HALF), bf16),
            vmem((CHIPS, 2 * TOKENS, HALF), bf16),
            vmem((CHIPS, 2, TOKENS, HIDDEN), bf16),
            vmem(rows, bf16),
            vmem(rows, bf16),
            vmem(rows, bf16),
            vmem(rows, bf16),
            vmem(square, bf16),
            vmem(square, bf16),
            vmem(square, f32),
            vmem((8, 128), f32),
            vmem((8, 128), f32),
            vmem(square, bf16),
            vmem(square, bf16),
            vmem(square, bf16),
            vmem(square, bf16),
            vmem(square, bf16),
            vmem(square, bf16),
            dma((2, EXP)),
            dma((2, EXP)),
            dma((CHIPS,)),
            dma((CHIPS, SIDES)),
            dma((CHIPS,)),
            dma((CHIPS,)),
            dma((CHIPS,)),
            dma((CHIPS,)),
            dma((CHIPS,)),
            dma((CHIPS,)),
            dma((CHIPS,)),
            dma((CHIPS,)),
            dma((CHIPS,)),
            dma((2,)),
            dma((2,)),
            dma((10,)),
        ],
        compiler_params=pltpu.CompilerParams(
            collective_id=0, has_side_effects=True, vmem_limit_bytes=60 << 20
        ),
        name="muon_owner",
    )(live, tok, cot, momentum)


def solution(mesh):
    in_specs = (
        P("rep", "exp", None, None, None),
        P("rep", "exp", None, None, None),
        P("rep", "exp", None),
        P("rep", "exp", None, None),
    )
    out_specs = (P("rep", "exp", None, None), P("rep", "exp", None, None))
    return jax.shard_map(
        on_device, mesh=mesh, in_specs=in_specs, out_specs=out_specs, check_vma=False
    )
```

```python
import functools
import math

import jax
import jax.numpy as jnp
from jax import lax
from jax.experimental import pallas as pl
from jax.experimental.pallas import tpu as pltpu
from jax.sharding import PartitionSpec as P

coef_a = 3.4445
coef_b = -4.775
coef_c = 2.0315
decay_rate = 0.95
norm_eps = 1e-07

REP = 16
EXP = 16
CHIPS = 8
YS = 4
EXPERTS_HERE = 4
SIDES = 2
SIDE_EXPERTS = EXPERTS_HERE // SIDES
SLOTS = 2
SIDE_ROWS = SIDE_EXPERTS * SLOTS
WIDTH = 2048
HALF = WIDTH // 2
SHARD = 128
HIDDEN = 768
TOKENS = 32
TILE = 256

MESH = pl.DeviceIdType.MESH
f32 = jnp.float32
bf16 = jnp.bfloat16


def remote(src, dst, send_sem, recv_sem, rep, exp):
    return pltpu.make_async_remote_copy(
        src_ref=src,
        dst_ref=dst,
        send_sem=send_sem,
        recv_sem=recv_sem,
        device_id=(rep, exp),
        device_id_type=MESH,
    )


def dot32(left, right):
    return jnp.dot(left, right, preferred_element_type=f32)


def dot_rows(left, right):
    return lax.dot_general(left, right, (((0,), (0,)), ((), ())), preferred_element_type=f32)


def kernel(
    counts,
    acts_hbm,
    cot_in,
    mom_hbm,
    new_mix,
    upd_mix,
    acts_in,
    mom_raw,
    mom_in,
    new_out,
    upd_out,
    tok_in,
    tok_r,
    t2_s,
    t2_r,
    cot_r,
    mom_r,
    new_s,
    nest_s,
    upd_s,
    gram_s,
    gram_r,
    gram_f,
    sq_s,
    sq_r,
    g0,
    bend0,
    step,
    g1,
    bend1,
    both,
    tok_ss,
    tok_rs,
    cot_ss,
    cot_rs,
    fwd_ss,
    mom_ss,
    mom_rs,
    t2_ss,
    t2_rs,
    new_ss,
    new_rs,
    upd_ss,
    upd_rs,
    pair_ss,
    pair_rs,
    local_sem,
):
    rep = lax.axis_index("rep")
    exp = lax.axis_index("exp")
    chip = rep // 2
    core = lax.rem(rep, 2)
    y = rep // 4
    x = lax.rem(chip, 2)
    peer = y * 2 + core
    rep_x = y * 4 + (1 - x) * 2 + core
    rep_core = chip * 2 + (1 - core)
    mine = 4 * x + y

    def matrix(of_chip):
        return 4 * lax.rem(of_chip, 2) + of_chip // 2

    def signal(to_rep, to_exp):
        pl.semaphore_signal(
            pltpu.get_barrier_semaphore(), inc=1, device_id=(to_rep, to_exp), device_id_type=MESH
        )

    def greet(i, carry):
        signal(rep, lax.rem(exp + i, EXP))
        signal(lax.rem(rep + i, REP), exp)
        signal(rep_x, lax.rem(exp + i, EXP))
        return carry

    lax.fori_loop(1, 16, greet, 0)
    acts_load = pltpu.make_async_copy(acts_hbm, acts_in, local_sem.at[6])
    mom_load = pltpu.make_async_copy(mom_hbm, mom_raw, local_sem.at[7])
    acts_load.start()
    mom_load.start()

    row = lax.broadcasted_iota(jnp.int32, (SIDE_ROWS, WIDTH), 0)

    def mask(i, carry):
        group = i // SIDES
        side = lax.rem(i, SIDES)
        at = i * SIDE_EXPERTS
        count = jnp.where(row < SLOTS, counts[at], counts[at + 1])
        values = acts_in[pl.ds(at, SIDE_EXPERTS)].astype(f32).reshape(SIDE_ROWS, WIDTH)
        tok_in[group, side] = jnp.where(lax.rem(row, SLOTS) < count, values, 0.0).astype(bf16)
        return carry

    acts_load.wait()
    lax.fori_loop(0, EXP * SIDES, mask, 0)
    pl.semaphore_wait(pltpu.get_barrier_semaphore(), 45)

    def tok_copy(i, other):
        to = lax.rem(exp + i, EXP)
        return remote(
            tok_in.at[to, 1 - x if other else x],
            tok_r.at[x, exp],
            tok_ss.at[other, i],
            tok_rs.at[x, exp],
            rep_x if other else rep,
            to,
        )

    def cot_copy(i):
        to = lax.rem(chip + i, CHIPS)
        return remote(
            cot_in.at[matrix(to)],
            cot_r.at[peer, x],
            cot_ss.at[i],
            cot_rs.at[peer, x],
            to * 2 + core,
            exp,
        )

    def mom_copy(i):
        to = lax.rem(chip + i, CHIPS)
        return remote(
            mom_in.at[matrix(to)],
            mom_r.at[chip],
            mom_ss.at[i],
            mom_rs.at[chip],
            to * 2 + core,
            exp,
        )

    tok_local = pltpu.make_async_copy(tok_in.at[exp, x], tok_r.at[x, exp], local_sem.at[0])
    cot_local = pltpu.make_async_copy(cot_in.at[mine], cot_r.at[peer, x], local_sem.at[1])
    mom_local = pltpu.make_async_copy(mom_in.at[mine], mom_r.at[chip], local_sem.at[2])

    tok_copy(0, 1).start()

    def start_tok(i, carry):
        tok_copy(i, 0).start()
        tok_copy(i, 1).start()
        return carry

    lax.fori_loop(1, EXP, start_tok, 0)

    def start_cot(i, carry):
        cot_copy(i).start()
        return carry

    lax.fori_loop(1, CHIPS, start_cot, 0)

    mom_load.wait()
    for expert in range(EXPERTS_HERE):
        mom_in[2 * expert : 2 * expert + 2] = jnp.swapaxes(mom_raw[:, expert], 0, 1)

    def start_mom(i, carry):
        mom_copy(i).start()
        return carry

    lax.fori_loop(1, CHIPS, start_mom, 0)
    tok_local.start()
    cot_local.start()
    mom_local.start()

    out_row = lax.broadcasted_iota(jnp.int32, (SHARD, SHARD), 0)
    in_row = lax.broadcasted_iota(jnp.int32, (SHARD, SHARD), 1)
    wanted = (
        lax.rem(out_row // SLOTS, SIDES * EXP) * SIDE_ROWS
        + (out_row // (SIDES * TOKENS)) * SLOTS
        + lax.rem(out_row, SLOTS)
    )
    order = jnp.where(in_row == wanted, 1.0, 0.0).astype(bf16)

    def wait_tok(i, carry):
        source = lax.rem(exp + i, EXP)
        remote(
            tok_in.at[0, 0], tok_r.at[x, source], tok_ss.at[0, i], tok_rs.at[x, source], rep, source
        ).wait_recv()
        return carry

    lax.fori_loop(1, EXP, wait_tok, 0)

    def wait_tok_x(i, carry):
        source = lax.rem(exp + i, EXP)
        remote(
            tok_in.at[0, 0],
            tok_r.at[1 - x, source],
            tok_ss.at[1, i],
            tok_rs.at[1 - x, source],
            rep_x,
            source,
        ).wait_recv()
        return carry

    lax.fori_loop(0, EXP, wait_tok_x, 0)
    tok_local.wait()

    rows = tok_r[...].reshape(SIDES * EXP * SIDE_ROWS, WIDTH)
    for piece in range(REP):
        part = dot32(order, rows[:, piece * SHARD : (piece + 1) * SHARD]).astype(bf16)
        for expert in range(SIDE_EXPERTS):
            t2_s[expert, piece % 2, :, (piece // 2) * SHARD : (piece // 2 + 1) * SHARD] = part[
                expert * SIDES * TOKENS : (expert + 1) * SIDES * TOKENS
            ]

    def t2_copy(i):
        to = lax.rem(peer + i, CHIPS)
        return remote(
            t2_s.at[to // 4, lax.rem(to, 2)],
            t2_r.at[peer],
            t2_ss.at[i],
            t2_rs.at[peer],
            (to // 2) * 4 + x * 2 + lax.rem(to, 2),
            exp,
        )

    def start_t2(i, carry):
        t2_copy(i).start()
        return carry

    lax.fori_loop(1, CHIPS, start_t2, 0)
    t2_local = pltpu.make_async_copy(t2_s.at[y // 2, core], t2_r.at[peer], local_sem.at[3])
    t2_local.start()

    def forward(of_chip):
        at = (of_chip // 2) * 2 + core
        side = lax.rem(of_chip, 2)
        return remote(
            cot_r.at[at, side],
            cot_r.at[at, side],
            fwd_ss.at[of_chip],
            cot_rs.at[at, side],
            rep_core,
            exp,
        )

    def wait_cot(i, carry):
        source = lax.rem(chip + i, CHIPS)
        at = (source // 2) * 2 + core
        side = lax.rem(source, 2)
        remote(
            cot_in.at[0],
            cot_r.at[at, side],
            cot_ss.at[i],
            cot_rs.at[at, side],
            source * 2 + core,
            exp,
        ).wait_recv()
        forward(source).start()
        return carry

    cot_local.wait()
    forward(chip).start()
    lax.fori_loop(1, CHIPS, wait_cot, 0)

    def wait_forward(i, carry):
        at = (i // 2) * 2 + 1 - core
        side = lax.rem(i, 2)
        remote(
            cot_r.at[at, side],
            cot_r.at[at, side],
            fwd_ss.at[i],
            cot_rs.at[at, side],
            rep_core,
            exp,
        ).wait_recv()
        return carry

    lax.fori_loop(0, CHIPS, wait_forward, 0)

    def wait_mom(source):
        remote(
            mom_in.at[0],
            mom_r.at[source],
            mom_ss.at[0],
            mom_rs.at[source],
            source * 2 + core,
            exp,
        ).wait_recv()

    def wait_t2(i, carry):
        source = lax.rem(peer + i, CHIPS)
        remote(
            t2_s.at[0],
            t2_r.at[source],
            t2_ss.at[i],
            t2_rs.at[source],
            (source // 2) * 4 + x * 2 + lax.rem(source, 2),
            exp,
        ).wait_recv()
        return carry

    lax.fori_loop(1, CHIPS, wait_t2, 0)
    t2_local.wait()

    def new_copy(i):
        to = lax.rem(chip + i, CHIPS)
        return remote(
            new_s.at[to], new_out.at[mine], new_ss.at[i], new_rs.at[mine], to * 2 + core, exp
        )

    sq_s[...] = jnp.zeros_like(sq_s)
    cots = cot_r[...].reshape(REP * TOKENS, HIDDEN)

    def gradient(i):
        at = lax.rem(chip + i, CHIPS)
        columns = pl.ds(pl.multiple_of(at * SHARD, SHARD), SHARD)
        feats = t2_r[:, :, columns].reshape(REP * TOKENS, SHARD)
        grad = dot_rows(feats, cots)
        mom = decay_rate * mom_r[at].astype(f32) + grad
        new_s[at] = mom.astype(bf16)
        nest = (grad + decay_rate * mom).astype(bf16)
        nest_s[at] = nest
        wide = nest.astype(f32)
        squares = jnp.sum((wide * wide).reshape(SHARD // 8, 8, HIDDEN // 128, 128), axis=(0, 2))
        sq_s[...] += squares

    def gradient_send(i, carry):
        wait_mom(lax.rem(chip + i, CHIPS))
        gradient(i)
        new_copy(i).start()
        return carry

    lax.fori_loop(1, CHIPS, gradient_send, 0)
    mom_local.wait()
    gradient(0)
    new_local = pltpu.make_async_copy(new_s.at[chip], new_out.at[mine], local_sem.at[4])
    new_local.start()

    def gram_tile(j, carry):
        columns = pl.ds(pl.multiple_of(j * TILE, TILE), TILE)
        values = nest_s[...].reshape(CHIPS * SHARD, HIDDEN)
        tile = dot_rows(values, nest_s[:, :, columns].reshape(CHIPS * SHARD, TILE))
        gram_f[:, columns] = tile
        gram_s[:, columns] = tile.astype(bf16)
        return carry

    lax.fori_loop(0, HIDDEN // TILE, gram_tile, 0)
    swap_gram = remote(gram_s, gram_r, pair_ss.at[0], pair_rs.at[0], rep_core, exp)
    swap_sq = remote(sq_s, sq_r, pair_ss.at[1], pair_rs.at[1], rep_core, exp)
    swap_gram.start()
    swap_sq.start()
    swap_sq.wait()
    swap_gram.wait()

    total = jnp.sum(jnp.sum(sq_s[...] + sq_r[...], axis=0, keepdims=True), axis=1, keepdims=True)
    inverse = 1.0 / (jnp.sqrt(total) + norm_eps)
    g0[...] = ((gram_f[...] + gram_r[...].astype(f32)) * inverse * inverse).astype(bf16)

    def tiles(body):
        def one(j, carry):
            body(pl.ds(pl.multiple_of(j * TILE, TILE), TILE))
            return carry

        lax.fori_loop(0, HIDDEN // TILE, one, 0)

    def bend0_tile(at):
        bend0[:, at] = (
            coef_b * g0[:, at].astype(f32) + coef_c * dot32(g0[...], g0[:, at])
        ).astype(bf16)

    def step_tile(at):
        step[:, at] = (
            coef_a * g0[:, at].astype(f32) + dot32(g0[...], bend0[:, at])
        ).astype(bf16)

    def g1_tile(at):
        g1[:, at] = (
            coef_a * step[:, at].astype(f32) + dot32(bend0[...], step[:, at])
        ).astype(bf16)

    def bend1_tile(at):
        bend1[:, at] = (
            coef_b * g1[:, at].astype(f32) + coef_c * dot32(g1[...], g1[:, at])
        ).astype(bf16)

    def both_tile(at):
        both[:, at] = (
            coef_a * (bend0[:, at].astype(f32) + bend1[:, at].astype(f32))
            + dot32(bend0[...], bend1[:, at])
        ).astype(bf16)

    for body in (bend0_tile, step_tile, g1_tile, bend1_tile, both_tile):
        tiles(body)

    scale = math.sqrt(WIDTH) * inverse

    def upd_copy(i):
        to = lax.rem(chip + i, CHIPS)
        return remote(
            upd_s.at[to], upd_out.at[mine], upd_ss.at[i], upd_rs.at[mine], to * 2 + core, exp
        )

    def turn(i):
        at = lax.rem(chip + i, CHIPS)
        rows = nest_s[at]
        turned = coef_a * coef_a * rows.astype(f32) + dot32(rows, both[...])
        upd_s[at] = (turned * scale).astype(bf16)

    def turn_send(i, carry):
        turn(i)
        upd_copy(i).start()
        return carry

    lax.fori_loop(1, CHIPS, turn_send, 0)
    turn(0)
    upd_local = pltpu.make_async_copy(upd_s.at[chip], upd_out.at[mine], local_sem.at[5])
    upd_local.start()

    def wait_new(i, carry):
        source = lax.rem(chip + i, CHIPS)
        remote(
            new_s.at[0],
            new_out.at[matrix(source)],
            new_ss.at[i],
            new_rs.at[matrix(source)],
            source * 2 + core,
            exp,
        ).wait_recv()
        return carry

    lax.fori_loop(1, CHIPS, wait_new, 0)
    new_local.wait()

    mix = jnp.where(
        out_row == lax.rem(in_row, SHARD // 2) * 2 + in_row // (SHARD // 2), 1.0, 0.0
    ).astype(bf16)

    def interleave(source, target, expert):
        for part in range(2):
            half = slice(part * (SHARD // 2), (part + 1) * (SHARD // 2))
            pair = jnp.concatenate(
                [source[2 * expert, half], source[2 * expert + 1, half]], axis=0
            )
            target[half, expert] = (
                dot32(mix, pair).astype(bf16).reshape(SHARD // 2, 2, HIDDEN)
            )

    for expert in range(EXPERTS_HERE):
        interleave(new_out, new_mix, expert)

    tok_copy(0, 1).wait_send()

    def finish_tok(i, carry):
        tok_copy(i, 0).wait_send()
        tok_copy(i, 1).wait_send()
        return carry

    lax.fori_loop(1, EXP, finish_tok, 0)

    forward(chip).wait_send()

    def finish(i, carry):
        cot_copy(i).wait_send()
        forward(lax.rem(chip + i, CHIPS)).wait_send()
        mom_copy(i).wait_send()
        t2_copy(i).wait_send()
        new_copy(i).wait_send()
        return carry

    lax.fori_loop(1, CHIPS, finish, 0)
    def collect(i, carry):
        side = lax.rem(x + i // 2, 2)
        half = lax.rem(y // 2 + i, 2)
        for kind in range(2):
            source = 2 * (2 * half + kind) + side

            @pl.when(source == chip)
            def _():
                upd_local.wait()

            @pl.when(source != chip)
            def _():
                remote(
                    upd_s.at[0],
                    upd_out.at[matrix(source)],
                    upd_ss.at[0],
                    upd_rs.at[matrix(source)],
                    source * 2 + core,
                    exp,
                ).wait_recv()

        interleave(upd_out, upd_mix, 2 * side + half)
        return carry

    lax.fori_loop(0, EXPERTS_HERE, collect, 0)

    def finish_upd(i, carry):
        upd_copy(i).wait_send()
        return carry

    lax.fori_loop(1, CHIPS, finish_upd, 0)


def on_device(acts, cotangent, counts, momentum):
    live = counts.reshape(EXP * EXPERTS_HERE)
    tok = acts.reshape(EXP * EXPERTS_HERE, SLOTS, WIDTH)
    cot = cotangent.reshape(CHIPS, TOKENS, HIDDEN)
    vmem = pltpu.VMEM
    dma = pltpu.SemaphoreType.DMA
    square = (HIDDEN, HIDDEN)
    rows = (CHIPS, SHARD, HIDDEN)
    mixed = (SHARD, EXPERTS_HERE, 2, HIDDEN)
    return pl.pallas_call(
        kernel,
        out_shape=(pltpu.VMEM(mixed, bf16),) * 2,
        in_specs=[
            pl.BlockSpec(memory_space=pltpu.SMEM),
            pl.BlockSpec(memory_space=pl.ANY),
            pl.BlockSpec(memory_space=pl.ANY),
            pl.BlockSpec(memory_space=pl.ANY),
        ],
        out_specs=(pl.BlockSpec(memory_space=pltpu.VMEM),) * 2,
        scratch_shapes=[
            vmem((EXP * EXPERTS_HERE, SLOTS, WIDTH), bf16),
            vmem(mixed, bf16),
            vmem(rows, bf16),
            vmem(rows, bf16),
            vmem(rows, bf16),
            vmem((EXP, SIDES, SIDE_ROWS, WIDTH), bf16),
            vmem((SIDES, EXP, SIDE_ROWS, WIDTH), bf16),
            vmem((SIDE_EXPERTS, 2, SIDES * TOKENS, HALF), bf16),
            vmem((CHIPS, 2 * TOKENS, HALF), bf16),
            vmem((CHIPS, 2, TOKENS, HIDDEN), bf16),
            vmem(rows, bf16),
            vmem(rows, bf16),
            vmem(rows, bf16),
            vmem(rows, bf16),
            vmem(square, bf16),
            vmem(square, bf16),
            vmem(square, f32),
            vmem((8, 128), f32),
            vmem((8, 128), f32),
            vmem(square, bf16),
            vmem(square, bf16),
            vmem(square, bf16),
            vmem(square, bf16),
            vmem(square, bf16),
            vmem(square, bf16),
            dma((2, EXP)),
            dma((2, EXP)),
            dma((CHIPS,)),
            dma((CHIPS, SIDES)),
            dma((CHIPS,)),
            dma((CHIPS,)),
            dma((CHIPS,)),
            dma((CHIPS,)),
            dma((CHIPS,)),
            dma((CHIPS,)),
            dma((CHIPS,)),
            dma((CHIPS,)),
            dma((CHIPS,)),
            dma((2,)),
            dma((2,)),
            dma((8,)),
        ],
        compiler_params=pltpu.CompilerParams(
            collective_id=0, has_side_effects=True, vmem_limit_bytes=60 << 20
        ),
        name="muon_owner",
    )(live, tok, cot, momentum)


def solution(mesh):
    in_specs = (
        P("rep", "exp", None, None, None),
        P("rep", "exp", None, None, None),
        P("rep", "exp", None),
        P("rep", "exp", None, None),
    )
    out_specs = (P("rep", "exp", None, None), P("rep", "exp", None, None))
    return jax.shard_map(
        on_device, mesh=mesh, in_specs=in_specs, out_specs=out_specs, check_vma=False
    )
```

```python
import functools
import math

import jax
import jax.numpy as jnp
from jax import lax
from jax.experimental import pallas as pl
from jax.experimental.pallas import tpu as pltpu
from jax.sharding import PartitionSpec as P

coef_a = 3.4445
coef_b = -4.775
coef_c = 2.0315
decay_rate = 0.95
norm_eps = 1e-07

REP = 16
EXP = 16
CHIPS = 8
YS = 4
EXPERTS_HERE = 4
SIDES = 2
SIDE_EXPERTS = EXPERTS_HERE // SIDES
SLOTS = 2
SIDE_ROWS = SIDE_EXPERTS * SLOTS
WIDTH = 2048
HALF = WIDTH // 2
SHARD = 128
HIDDEN = 768
TOKENS = 32
TILE = 256
EARLY = 4
LEADER = 0
MESSENGER = 1

MESH = pl.DeviceIdType.MESH
f32 = jnp.float32
bf16 = jnp.bfloat16


def remote(src, dst, send_sem, recv_sem, rep, exp):
    return pltpu.make_async_remote_copy(
        src_ref=src,
        dst_ref=dst,
        send_sem=send_sem,
        recv_sem=recv_sem,
        device_id=(rep, exp),
        device_id_type=MESH,
    )


def dot32(left, right):
    return jnp.dot(left, right, preferred_element_type=f32)


def dot_rows(left, right):
    return lax.dot_general(left, right, (((0,), (0,)), ((), ())), preferred_element_type=f32)


def kernel(
    counts,
    acts_hbm,
    cot_in,
    mom_hbm,
    new_mix,
    upd_mix,
    acts_in,
    mom_raw,
    mom_in,
    new_out,
    upd_out,
    tok_in,
    tok_r,
    t2_s,
    t2_r,
    cot_r,
    mom_r,
    new_s,
    nest_s,
    upd_s,
    gram_s,
    gram_r,
    gram_f,
    sq_s,
    sq_r,
    g0,
    bend0,
    step,
    g1,
    bend1,
    both,
    tok_ss,
    tok_rs,
    cot_ss,
    cot_rs,
    fwd_ss,
    mom_ss,
    mom_rs,
    t2_ss,
    t2_rs,
    new_ss,
    new_rs,
    upd_ss,
    upd_rs,
    pair_ss,
    pair_rs,
    local_sem,
    group_sem,
    all_sem,
):
    rep = lax.axis_index("rep")
    exp = lax.axis_index("exp")
    chip = rep // 2
    core = lax.rem(rep, 2)
    y = rep // 4
    x = lax.rem(chip, 2)
    peer = y * 2 + core
    rep_x = y * 4 + (1 - x) * 2 + core
    rep_core = chip * 2 + (1 - core)
    mine = 4 * x + y

    def matrix(of_chip):
        return 4 * lax.rem(of_chip, 2) + of_chip // 2

    def signal(to_rep, to_exp):
        pl.semaphore_signal(
            pltpu.get_barrier_semaphore(), inc=1, device_id=(to_rep, to_exp), device_id_type=MESH
        )

    @pl.when(rep != LEADER)
    def _():
        signal(LEADER, exp)

    near = jnp.where(rep == LEADER, MESSENGER, rep)
    cross = jnp.where(rep_x == LEADER, MESSENGER, rep_x)

    def greet(i, carry):
        to = lax.rem(exp + i, EXP)
        signal(near, to)
        signal(cross, to)
        return carry

    @pl.when(rep_x != LEADER)
    def _():
        signal(rep_x, exp)

    lax.fori_loop(1, EXP, greet, 0)
    acts_load = pltpu.make_async_copy(acts_hbm, acts_in, local_sem.at[6])
    mom_load = pltpu.make_async_copy(mom_hbm, mom_raw, local_sem.at[7])
    acts_load.start()
    mom_load.start()

    @pl.when(rep == LEADER)
    def _():
        pl.semaphore_wait(pltpu.get_barrier_semaphore(), REP - 1)

        def tell(i, carry):
            pl.semaphore_signal(
                group_sem, inc=1, device_id=(lax.rem(rep + i, REP), exp), device_id_type=MESH
            )
            return carry

        lax.fori_loop(1, REP, tell, 0)

    row = lax.broadcasted_iota(jnp.int32, (SIDE_ROWS, WIDTH), 0)

    def mask(i, carry):
        group = i // SIDES
        side = lax.rem(i, SIDES)
        at = i * SIDE_EXPERTS
        count = jnp.where(row < SLOTS, counts[at], counts[at + 1])
        values = acts_in[pl.ds(at, SIDE_EXPERTS)].astype(f32).reshape(SIDE_ROWS, WIDTH)
        tok_in[group, side] = jnp.where(lax.rem(row, SLOTS) < count, values, 0.0).astype(bf16)
        return carry

    acts_load.wait()
    lax.fori_loop(0, EXP * SIDES, mask, 0)
    mom_load.wait()
    for expert in range(EXPERTS_HERE):
        mom_in[2 * expert : 2 * expert + 2] = jnp.swapaxes(mom_raw[:, expert], 0, 1)

    def tok_copy(i, other):
        to = lax.rem(exp + i, EXP)
        return remote(
            tok_in.at[to, 1 - x if other else x],
            tok_r.at[x, exp],
            tok_ss.at[other, i],
            tok_rs.at[x, exp],
            rep_x if other else rep,
            to,
        )

    def cot_copy(i):
        to = lax.rem(chip + i, CHIPS)
        return remote(
            cot_in.at[matrix(to)],
            cot_r.at[peer, x],
            cot_ss.at[i],
            cot_rs.at[peer, x],
            to * 2 + core,
            exp,
        )

    def mom_copy(i):
        step, turned = (i, 1 - x) if i < YS else (i - YS + 1, x)
        to = 2 * lax.rem(y + step, YS) + turned
        return remote(
            mom_in.at[matrix(to)],
            mom_r.at[chip],
            mom_ss.at[i],
            mom_rs.at[chip],
            to * 2 + core,
            exp,
        )

    tok_local = pltpu.make_async_copy(tok_in.at[exp, x], tok_r.at[x, exp], local_sem.at[0])
    cot_local = pltpu.make_async_copy(cot_in.at[mine], cot_r.at[peer, x], local_sem.at[1])
    mom_local = pltpu.make_async_copy(mom_in.at[mine], mom_r.at[chip], local_sem.at[2])

    def start_cot(i, carry):
        cot_copy(i).start()
        return carry

    def hear_group(listens):
        @pl.when(listens)
        def _():
            pl.semaphore_wait(group_sem, 1)

        lax.fori_loop(1, CHIPS, start_cot, 0)

    early = exp // 2 < EARLY

    @pl.when(early)
    def _():
        hear_group(rep != LEADER)
        for i in range(4, 7):
            mom_copy(i).start()

    @pl.when(rep == LEADER)
    def _():
        pl.semaphore_wait(all_sem, 1)

    @pl.when(jnp.logical_and(rep == MESSENGER, jnp.logical_not(early)))
    def _():
        pl.semaphore_wait(group_sem, 1)

    @pl.when(rep == MESSENGER)
    def _():
        pl.semaphore_wait(pltpu.get_barrier_semaphore(), 4 * (EXP - 1) + 1)
        pl.semaphore_signal(all_sem, inc=1, device_id=(LEADER, exp), device_id_type=MESH)

    @pl.when(jnp.logical_and(rep != LEADER, rep != MESSENGER))
    def _():
        pl.semaphore_wait(pltpu.get_barrier_semaphore(), 2 * (EXP - 1) + 1)

    tok_copy(0, 1).start()

    def start_tok(i, carry):
        tok_copy(i, 0).start()
        tok_copy(i, 1).start()
        return carry

    lax.fori_loop(1, EXP, start_tok, 0)

    @pl.when(jnp.logical_not(early))
    def _():
        hear_group(jnp.logical_and(rep != LEADER, rep != MESSENGER))
        for i in range(4, 7):
            mom_copy(i).start()

    for i in range(4):
        mom_copy(i).start()

    tok_local.start()
    cot_local.start()
    mom_local.start()

    out_row = lax.broadcasted_iota(jnp.int32, (SHARD, SHARD), 0)
    in_row = lax.broadcasted_iota(jnp.int32, (SHARD, SHARD), 1)
    wanted = (
        lax.rem(out_row // SLOTS, SIDES * EXP) * SIDE_ROWS
        + (out_row // (SIDES * TOKENS)) * SLOTS
        + lax.rem(out_row, SLOTS)
    )
    order = jnp.where(in_row == wanted, 1.0, 0.0).astype(bf16)

    def wait_tok(i, carry):
        source = lax.rem(exp + i, EXP)
        remote(
            tok_in.at[0, 0], tok_r.at[x, source], tok_ss.at[0, i], tok_rs.at[x, source], rep, source
        ).wait_recv()
        return carry

    lax.fori_loop(1, EXP, wait_tok, 0)

    def wait_tok_x(i, carry):
        source = lax.rem(exp + i, EXP)
        remote(
            tok_in.at[0, 0],
            tok_r.at[1 - x, source],
            tok_ss.at[1, i],
            tok_rs.at[1 - x, source],
            rep_x,
            source,
        ).wait_recv()
        return carry

    lax.fori_loop(0, EXP, wait_tok_x, 0)
    tok_local.wait()

    rows = tok_r[...].reshape(SIDES * EXP * SIDE_ROWS, WIDTH)
    for piece in range(REP):
        part = dot32(order, rows[:, piece * SHARD : (piece + 1) * SHARD]).astype(bf16)
        for expert in range(SIDE_EXPERTS):
            t2_s[expert, piece % 2, :, (piece // 2) * SHARD : (piece // 2 + 1) * SHARD] = part[
                expert * SIDES * TOKENS : (expert + 1) * SIDES * TOKENS
            ]

    def t2_copy(i):
        to = lax.rem(peer + i, CHIPS)
        return remote(
            t2_s.at[to // 4, lax.rem(to, 2)],
            t2_r.at[peer],
            t2_ss.at[i],
            t2_rs.at[peer],
            (to // 2) * 4 + x * 2 + lax.rem(to, 2),
            exp,
        )

    def start_t2(i, carry):
        t2_copy(i).start()
        return carry

    lax.fori_loop(1, CHIPS, start_t2, 0)
    t2_local = pltpu.make_async_copy(t2_s.at[y // 2, core], t2_r.at[peer], local_sem.at[3])
    t2_local.start()

    def forward(of_chip):
        at = (of_chip // 2) * 2 + core
        side = lax.rem(of_chip, 2)
        return remote(
            cot_r.at[at, side],
            cot_r.at[at, side],
            fwd_ss.at[of_chip],
            cot_rs.at[at, side],
            rep_core,
            exp,
        )

    def wait_cot(i, carry):
        source = lax.rem(chip + i, CHIPS)
        at = (source // 2) * 2 + core
        side = lax.rem(source, 2)
        remote(
            cot_in.at[0],
            cot_r.at[at, side],
            cot_ss.at[i],
            cot_rs.at[at, side],
            source * 2 + core,
            exp,
        ).wait_recv()
        forward(source).start()
        return carry

    cot_local.wait()
    forward(chip).start()
    lax.fori_loop(1, CHIPS, wait_cot, 0)

    def wait_forward(i, carry):
        at = (i // 2) * 2 + 1 - core
        side = lax.rem(i, 2)
        remote(
            cot_r.at[at, side],
            cot_r.at[at, side],
            fwd_ss.at[i],
            cot_rs.at[at, side],
            rep_core,
            exp,
        ).wait_recv()
        return carry

    lax.fori_loop(0, CHIPS, wait_forward, 0)

    def wait_mom(source):
        remote(
            mom_in.at[0],
            mom_r.at[source],
            mom_ss.at[0],
            mom_rs.at[source],
            source * 2 + core,
            exp,
        ).wait_recv()

    def wait_t2(i, carry):
        source = lax.rem(peer + i, CHIPS)
        remote(
            t2_s.at[0],
            t2_r.at[source],
            t2_ss.at[i],
            t2_rs.at[source],
            (source // 2) * 4 + x * 2 + lax.rem(source, 2),
            exp,
        ).wait_recv()
        return carry

    lax.fori_loop(1, CHIPS, wait_t2, 0)
    t2_local.wait()

    def new_copy(i):
        to = lax.rem(chip + i, CHIPS)
        return remote(
            new_s.at[to], new_out.at[mine], new_ss.at[i], new_rs.at[mine], to * 2 + core, exp
        )

    sq_s[...] = jnp.zeros_like(sq_s)
    cots = cot_r[...].reshape(REP * TOKENS, HIDDEN)

    def gradient(i):
        at = lax.rem(chip + i, CHIPS)
        columns = pl.ds(pl.multiple_of(at * SHARD, SHARD), SHARD)
        feats = t2_r[:, :, columns].reshape(REP * TOKENS, SHARD)
        grad = dot_rows(feats, cots)
        mom = decay_rate * mom_r[at].astype(f32) + grad
        new_s[at] = mom.astype(bf16)
        nest = (grad + decay_rate * mom).astype(bf16)
        nest_s[at] = nest
        wide = nest.astype(f32)
        squares = jnp.sum((wide * wide).reshape(SHARD // 8, 8, HIDDEN // 128, 128), axis=(0, 2))
        sq_s[...] += squares

    def gradient_send(i, carry):
        wait_mom(lax.rem(chip + i, CHIPS))
        gradient(i)
        new_copy(i).start()
        return carry

    lax.fori_loop(1, CHIPS, gradient_send, 0)
    mom_local.wait()
    gradient(0)
    new_local = pltpu.make_async_copy(new_s.at[chip], new_out.at[mine], local_sem.at[4])
    new_local.start()

    def gram_tile(j, carry):
        columns = pl.ds(pl.multiple_of(j * TILE, TILE), TILE)
        values = nest_s[...].reshape(CHIPS * SHARD, HIDDEN)
        tile = dot_rows(values, nest_s[:, :, columns].reshape(CHIPS * SHARD, TILE))
        gram_f[:, columns] = tile
        gram_s[:, columns] = tile.astype(bf16)
        return carry

    lax.fori_loop(0, HIDDEN // TILE, gram_tile, 0)
    swap_gram = remote(gram_s, gram_r, pair_ss.at[0], pair_rs.at[0], rep_core, exp)
    swap_sq = remote(sq_s, sq_r, pair_ss.at[1], pair_rs.at[1], rep_core, exp)
    swap_gram.start()
    swap_sq.start()
    swap_sq.wait()
    swap_gram.wait()

    total = jnp.sum(jnp.sum(sq_s[...] + sq_r[...], axis=0, keepdims=True), axis=1, keepdims=True)
    inverse = 1.0 / (jnp.sqrt(total) + norm_eps)
    g0[...] = ((gram_f[...] + gram_r[...].astype(f32)) * inverse * inverse).astype(bf16)

    def tiles(body):
        def one(j, carry):
            body(pl.ds(pl.multiple_of(j * TILE, TILE), TILE))
            return carry

        lax.fori_loop(0, HIDDEN // TILE, one, 0)

    def bend0_tile(at):
        bend0[:, at] = (
            coef_b * g0[:, at].astype(f32) + coef_c * dot32(g0[...], g0[:, at])
        ).astype(bf16)

    def step_tile(at):
        step[:, at] = (
            coef_a * g0[:, at].astype(f32) + dot32(g0[...], bend0[:, at])
        ).astype(bf16)

    def g1_tile(at):
        g1[:, at] = (
            coef_a * step[:, at].astype(f32) + dot32(bend0[...], step[:, at])
        ).astype(bf16)

    def bend1_tile(at):
        bend1[:, at] = (
            coef_b * g1[:, at].astype(f32) + coef_c * dot32(g1[...], g1[:, at])
        ).astype(bf16)

    def both_tile(at):
        both[:, at] = (
            coef_a * (bend0[:, at].astype(f32) + bend1[:, at].astype(f32))
            + dot32(bend0[...], bend1[:, at])
        ).astype(bf16)

    for body in (bend0_tile, step_tile, g1_tile, bend1_tile, both_tile):
        tiles(body)

    scale = math.sqrt(WIDTH) * inverse

    def upd_copy(i):
        to = lax.rem(chip + i, CHIPS)
        return remote(
            upd_s.at[to], upd_out.at[mine], upd_ss.at[i], upd_rs.at[mine], to * 2 + core, exp
        )

    def turn(i):
        at = lax.rem(chip + i, CHIPS)
        rows = nest_s[at]
        turned = coef_a * coef_a * rows.astype(f32) + dot32(rows, both[...])
        upd_s[at] = (turned * scale).astype(bf16)

    def turn_send(i, carry):
        turn(i)
        upd_copy(i).start()
        return carry

    lax.fori_loop(1, CHIPS, turn_send, 0)
    turn(0)
    upd_local = pltpu.make_async_copy(upd_s.at[chip], upd_out.at[mine], local_sem.at[5])
    upd_local.start()

    def wait_new(i, carry):
        source = lax.rem(chip + i, CHIPS)
        remote(
            new_s.at[0],
            new_out.at[matrix(source)],
            new_ss.at[i],
            new_rs.at[matrix(source)],
            source * 2 + core,
            exp,
        ).wait_recv()
        return carry

    lax.fori_loop(1, CHIPS, wait_new, 0)
    new_local.wait()

    mix = jnp.where(
        out_row == lax.rem(in_row, SHARD // 2) * 2 + in_row // (SHARD // 2), 1.0, 0.0
    ).astype(bf16)

    def interleave(source, target, expert):
        for part in range(2):
            half = slice(part * (SHARD // 2), (part + 1) * (SHARD // 2))
            pair = jnp.concatenate(
                [source[2 * expert, half], source[2 * expert + 1, half]], axis=0
            )
            target[half, expert] = (
                dot32(mix, pair).astype(bf16).reshape(SHARD // 2, 2, HIDDEN)
            )

    for expert in range(EXPERTS_HERE):
        interleave(new_out, new_mix, expert)

    tok_copy(0, 1).wait_send()

    def finish_tok(i, carry):
        tok_copy(i, 0).wait_send()
        tok_copy(i, 1).wait_send()
        return carry

    lax.fori_loop(1, EXP, finish_tok, 0)

    forward(chip).wait_send()
    for i in range(7):
        mom_copy(i).wait_send()

    def finish(i, carry):
        cot_copy(i).wait_send()
        forward(lax.rem(chip + i, CHIPS)).wait_send()
        t2_copy(i).wait_send()
        new_copy(i).wait_send()
        return carry

    lax.fori_loop(1, CHIPS, finish, 0)
    def collect(i, carry):
        side = lax.rem(x + i // 2, 2)
        half = lax.rem(y // 2 + i, 2)
        for kind in range(2):
            source = 2 * (2 * half + kind) + side

            @pl.when(source == chip)
            def _():
                upd_local.wait()

            @pl.when(source != chip)
            def _():
                remote(
                    upd_s.at[0],
                    upd_out.at[matrix(source)],
                    upd_ss.at[0],
                    upd_rs.at[matrix(source)],
                    source * 2 + core,
                    exp,
                ).wait_recv()

        interleave(upd_out, upd_mix, 2 * side + half)
        return carry

    lax.fori_loop(0, EXPERTS_HERE, collect, 0)

    def finish_upd(i, carry):
        upd_copy(i).wait_send()
        return carry

    lax.fori_loop(1, CHIPS, finish_upd, 0)


def on_device(acts, cotangent, counts, momentum):
    live = counts.reshape(EXP * EXPERTS_HERE)
    tok = acts.reshape(EXP * EXPERTS_HERE, SLOTS, WIDTH)
    cot = cotangent.reshape(CHIPS, TOKENS, HIDDEN)
    vmem = pltpu.VMEM
    dma = pltpu.SemaphoreType.DMA
    square = (HIDDEN, HIDDEN)
    rows = (CHIPS, SHARD, HIDDEN)
    mixed = (SHARD, EXPERTS_HERE, 2, HIDDEN)
    return pl.pallas_call(
        kernel,
        out_shape=(pltpu.VMEM(mixed, bf16),) * 2,
        in_specs=[
            pl.BlockSpec(memory_space=pltpu.SMEM),
            pl.BlockSpec(memory_space=pl.ANY),
            pl.BlockSpec(memory_space=pl.ANY),
            pl.BlockSpec(memory_space=pl.ANY),
        ],
        out_specs=(pl.BlockSpec(memory_space=pltpu.VMEM),) * 2,
        scratch_shapes=[
            vmem((EXP * EXPERTS_HERE, SLOTS, WIDTH), bf16),
            vmem(mixed, bf16),
            vmem(rows, bf16),
            vmem(rows, bf16),
            vmem(rows, bf16),
            vmem((EXP, SIDES, SIDE_ROWS, WIDTH), bf16),
            vmem((SIDES, EXP, SIDE_ROWS, WIDTH), bf16),
            vmem((SIDE_EXPERTS, 2, SIDES * TOKENS, HALF), bf16),
            vmem((CHIPS, 2 * TOKENS, HALF), bf16),
            vmem((CHIPS, 2, TOKENS, HIDDEN), bf16),
            vmem(rows, bf16),
            vmem(rows, bf16),
            vmem(rows, bf16),
            vmem(rows, bf16),
            vmem(square, bf16),
            vmem(square, bf16),
            vmem(square, f32),
            vmem((8, 128), f32),
            vmem((8, 128), f32),
            vmem(square, bf16),
            vmem(square, bf16),
            vmem(square, bf16),
            vmem(square, bf16),
            vmem(square, bf16),
            vmem(square, bf16),
            dma((2, EXP)),
            dma((2, EXP)),
            dma((CHIPS,)),
            dma((CHIPS, SIDES)),
            dma((CHIPS,)),
            dma((CHIPS,)),
            dma((CHIPS,)),
            dma((CHIPS,)),
            dma((CHIPS,)),
            dma((CHIPS,)),
            dma((CHIPS,)),
            dma((CHIPS,)),
            dma((CHIPS,)),
            dma((2,)),
            dma((2,)),
            dma((8,)),
            pltpu.SemaphoreType.REGULAR,
            pltpu.SemaphoreType.REGULAR,
        ],
        compiler_params=pltpu.CompilerParams(
            collective_id=0, has_side_effects=True, vmem_limit_bytes=60 << 20
        ),
        name="muon_owner",
    )(live, tok, cot, momentum)


def solution(mesh):
    in_specs = (
        P("rep", "exp", None, None, None),
        P("rep", "exp", None, None, None),
        P("rep", "exp", None),
        P("rep", "exp", None, None),
    )
    out_specs = (P("rep", "exp", None, None), P("rep", "exp", None, None))
    return jax.shard_map(
        on_device, mesh=mesh, in_specs=in_specs, out_specs=out_specs, check_vma=False
    )
```

```python
import functools
import math

import jax
import jax.numpy as jnp
from jax import lax
from jax.experimental import pallas as pl
from jax.experimental.pallas import tpu as pltpu
from jax.sharding import PartitionSpec as P

coef_a = 3.4445
coef_b = -4.775
coef_c = 2.0315
decay_rate = 0.95
norm_eps = 1e-07

REP = 16
EXP = 16
CHIPS = 8
YS = 4
EXPERTS_HERE = 4
SIDES = 2
SIDE_EXPERTS = EXPERTS_HERE // SIDES
SLOTS = 2
SIDE_ROWS = SIDE_EXPERTS * SLOTS
WIDTH = 2048
HALF = WIDTH // 2
SHARD = 128
HIDDEN = 768
TOKENS = 32
TILE = 256
EARLY = 4
LEADER = 0
MESSENGER = 1

MESH = pl.DeviceIdType.MESH
f32 = jnp.float32
bf16 = jnp.bfloat16


def remote(src, dst, send_sem, recv_sem, rep, exp):
    return pltpu.make_async_remote_copy(
        src_ref=src,
        dst_ref=dst,
        send_sem=send_sem,
        recv_sem=recv_sem,
        device_id=(rep, exp),
        device_id_type=MESH,
    )


def dot32(left, right):
    return jnp.dot(left, right, preferred_element_type=f32)


def dot_rows(left, right):
    return lax.dot_general(left, right, (((0,), (0,)), ((), ())), preferred_element_type=f32)


def kernel(
    counts,
    acts_hbm,
    cot_in,
    mom_hbm,
    new_mix,
    upd_mix,
    acts_in,
    mom_raw,
    mom_in,
    new_out,
    upd_out,
    tok_in,
    tok_r,
    t2_s,
    t2_r,
    cot_r,
    mom_r,
    new_s,
    nest_s,
    upd_s,
    gram_s,
    gram_r,
    gram_f,
    sq_s,
    sq_r,
    g0,
    bend0,
    step,
    g1,
    bend1,
    both,
    tok_ss,
    tok_rs,
    cot_ss,
    cot_rs,
    fwd_ss,
    mom_ss,
    mom_rs,
    t2_ss,
    t2_rs,
    new_ss,
    new_rs,
    upd_ss,
    upd_rs,
    pair_ss,
    pair_rs,
    local_sem,
    group_sem,
    all_sem,
):
    rep = lax.axis_index("rep")
    exp = lax.axis_index("exp")
    chip = rep // 2
    core = lax.rem(rep, 2)
    y = rep // 4
    x = lax.rem(chip, 2)
    peer = y * 2 + core
    rep_x = y * 4 + (1 - x) * 2 + core
    rep_core = chip * 2 + (1 - core)
    mine = 4 * x + y

    def matrix(of_chip):
        return 4 * lax.rem(of_chip, 2) + of_chip // 2

    def signal(to_rep, to_exp):
        pl.semaphore_signal(
            pltpu.get_barrier_semaphore(), inc=1, device_id=(to_rep, to_exp), device_id_type=MESH
        )

    acts_load = pltpu.make_async_copy(acts_hbm, acts_in, local_sem.at[6])
    mom_load = pltpu.make_async_copy(mom_hbm, mom_raw, local_sem.at[7])
    acts_load.start()
    mom_load.start()

    @pl.when(rep != LEADER)
    def _():
        signal(LEADER, exp)

    near = jnp.where(rep == LEADER, MESSENGER, rep)
    cross = jnp.where(rep_x == LEADER, MESSENGER, rep_x)

    def greet(i, carry):
        to = lax.rem(exp + i, EXP)
        signal(near, to)
        signal(cross, to)
        return carry

    @pl.when(rep_x != LEADER)
    def _():
        signal(rep_x, exp)

    lax.fori_loop(1, EXP, greet, 0)

    @pl.when(rep == LEADER)
    def _():
        pl.semaphore_wait(pltpu.get_barrier_semaphore(), REP - 1)

        def tell(i, carry):
            pl.semaphore_signal(
                group_sem, inc=1, device_id=(lax.rem(rep + i, REP), exp), device_id_type=MESH
            )
            return carry

        lax.fori_loop(1, REP, tell, 0)

    row = lax.broadcasted_iota(jnp.int32, (SIDE_ROWS, WIDTH), 0)

    def mask(i, carry):
        group = i // SIDES
        side = lax.rem(i, SIDES)
        at = i * SIDE_EXPERTS
        count = jnp.where(row < SLOTS, counts[at], counts[at + 1])
        values = acts_in[pl.ds(at, SIDE_EXPERTS)].astype(f32).reshape(SIDE_ROWS, WIDTH)
        tok_in[group, side] = jnp.where(lax.rem(row, SLOTS) < count, values, 0.0).astype(bf16)
        return carry

    acts_load.wait()
    lax.fori_loop(0, EXP * SIDES, mask, 0)
    def tok_copy(i, other):
        to = lax.rem(exp + i, EXP)
        return remote(
            tok_in.at[to, 1 - x if other else x],
            tok_r.at[x, exp],
            tok_ss.at[other, i],
            tok_rs.at[x, exp],
            rep_x if other else rep,
            to,
        )

    def cot_copy(i):
        to = lax.rem(chip + i, CHIPS)
        return remote(
            cot_in.at[matrix(to)],
            cot_r.at[peer, x],
            cot_ss.at[i],
            cot_rs.at[peer, x],
            to * 2 + core,
            exp,
        )

    def mom_copy(i):
        step, turned = (i, 1 - x) if i < YS else (i - YS + 1, x)
        to = 2 * lax.rem(y + step, YS) + turned
        return remote(
            mom_in.at[matrix(to)],
            mom_r.at[chip],
            mom_ss.at[i],
            mom_rs.at[chip],
            to * 2 + core,
            exp,
        )

    tok_local = pltpu.make_async_copy(tok_in.at[exp, x], tok_r.at[x, exp], local_sem.at[0])
    cot_local = pltpu.make_async_copy(cot_in.at[mine], cot_r.at[peer, x], local_sem.at[1])
    mom_local = pltpu.make_async_copy(mom_in.at[mine], mom_r.at[chip], local_sem.at[2])

    def start_cot(i, carry):
        cot_copy(i).start()
        return carry

    def hear_group(listens):
        @pl.when(listens)
        def _():
            pl.semaphore_wait(group_sem, 1)

        lax.fori_loop(1, CHIPS, start_cot, 0)

    def split_momentum():
        mom_load.wait()
        for expert in range(EXPERTS_HERE):
            mom_in[2 * expert : 2 * expert + 2] = jnp.swapaxes(mom_raw[:, expert], 0, 1)

    early = exp // 2 < EARLY

    @pl.when(early)
    def _():
        split_momentum()
        hear_group(rep != LEADER)
        for i in range(4, 7):
            mom_copy(i).start()

    @pl.when(rep == LEADER)
    def _():
        pl.semaphore_wait(all_sem, 1)

    @pl.when(jnp.logical_and(rep == MESSENGER, jnp.logical_not(early)))
    def _():
        pl.semaphore_wait(group_sem, 1)

    @pl.when(rep == MESSENGER)
    def _():
        pl.semaphore_wait(pltpu.get_barrier_semaphore(), 4 * (EXP - 1) + 1)
        pl.semaphore_signal(all_sem, inc=1, device_id=(LEADER, exp), device_id_type=MESH)

    @pl.when(jnp.logical_and(rep != LEADER, rep != MESSENGER))
    def _():
        pl.semaphore_wait(pltpu.get_barrier_semaphore(), 2 * (EXP - 1) + 1)

    tok_copy(0, 1).start()

    def start_tok(i, carry):
        tok_copy(i, 0).start()
        tok_copy(i, 1).start()
        return carry

    lax.fori_loop(1, EXP, start_tok, 0)

    @pl.when(jnp.logical_not(early))
    def _():
        hear_group(jnp.logical_and(rep != LEADER, rep != MESSENGER))
        split_momentum()
        for i in range(4, 7):
            mom_copy(i).start()

    for i in range(4):
        mom_copy(i).start()

    tok_local.start()
    cot_local.start()
    mom_local.start()

    out_row = lax.broadcasted_iota(jnp.int32, (SHARD, SHARD), 0)
    in_row = lax.broadcasted_iota(jnp.int32, (SHARD, SHARD), 1)
    wanted = (
        lax.rem(out_row // SLOTS, SIDES * EXP) * SIDE_ROWS
        + (out_row // (SIDES * TOKENS)) * SLOTS
        + lax.rem(out_row, SLOTS)
    )
    order = jnp.where(in_row == wanted, 1.0, 0.0).astype(bf16)

    def wait_tok(i, carry):
        source = lax.rem(exp + i, EXP)
        remote(
            tok_in.at[0, 0], tok_r.at[x, source], tok_ss.at[0, i], tok_rs.at[x, source], rep, source
        ).wait_recv()
        return carry

    lax.fori_loop(1, EXP, wait_tok, 0)

    def wait_tok_x(i, carry):
        source = lax.rem(exp + i, EXP)
        remote(
            tok_in.at[0, 0],
            tok_r.at[1 - x, source],
            tok_ss.at[1, i],
            tok_rs.at[1 - x, source],
            rep_x,
            source,
        ).wait_recv()
        return carry

    lax.fori_loop(0, EXP, wait_tok_x, 0)
    tok_local.wait()

    rows = tok_r[...].reshape(SIDES * EXP * SIDE_ROWS, WIDTH)
    for piece in range(REP):
        part = dot32(order, rows[:, piece * SHARD : (piece + 1) * SHARD]).astype(bf16)
        for expert in range(SIDE_EXPERTS):
            t2_s[expert, piece % 2, :, (piece // 2) * SHARD : (piece // 2 + 1) * SHARD] = part[
                expert * SIDES * TOKENS : (expert + 1) * SIDES * TOKENS
            ]

    def t2_copy(i):
        to = lax.rem(peer + i, CHIPS)
        return remote(
            t2_s.at[to // 4, lax.rem(to, 2)],
            t2_r.at[peer],
            t2_ss.at[i],
            t2_rs.at[peer],
            (to // 2) * 4 + x * 2 + lax.rem(to, 2),
            exp,
        )

    def start_t2(i, carry):
        t2_copy(i).start()
        return carry

    lax.fori_loop(1, CHIPS, start_t2, 0)
    t2_local = pltpu.make_async_copy(t2_s.at[y // 2, core], t2_r.at[peer], local_sem.at[3])
    t2_local.start()

    def forward(of_chip):
        at = (of_chip // 2) * 2 + core
        side = lax.rem(of_chip, 2)
        return remote(
            cot_r.at[at, side],
            cot_r.at[at, side],
            fwd_ss.at[of_chip],
            cot_rs.at[at, side],
            rep_core,
            exp,
        )

    def wait_cot(i, carry):
        source = lax.rem(chip + i, CHIPS)
        at = (source // 2) * 2 + core
        side = lax.rem(source, 2)
        remote(
            cot_in.at[0],
            cot_r.at[at, side],
            cot_ss.at[i],
            cot_rs.at[at, side],
            source * 2 + core,
            exp,
        ).wait_recv()
        forward(source).start()
        return carry

    cot_local.wait()
    forward(chip).start()
    lax.fori_loop(1, CHIPS, wait_cot, 0)

    def wait_forward(i, carry):
        at = (i // 2) * 2 + 1 - core
        side = lax.rem(i, 2)
        remote(
            cot_r.at[at, side],
            cot_r.at[at, side],
            fwd_ss.at[i],
            cot_rs.at[at, side],
            rep_core,
            exp,
        ).wait_recv()
        return carry

    lax.fori_loop(0, CHIPS, wait_forward, 0)

    def wait_mom(source):
        remote(
            mom_in.at[0],
            mom_r.at[source],
            mom_ss.at[0],
            mom_rs.at[source],
            source * 2 + core,
            exp,
        ).wait_recv()

    def wait_t2(i, carry):
        source = lax.rem(peer + i, CHIPS)
        remote(
            t2_s.at[0],
            t2_r.at[source],
            t2_ss.at[i],
            t2_rs.at[source],
            (source // 2) * 4 + x * 2 + lax.rem(source, 2),
            exp,
        ).wait_recv()
        return carry

    lax.fori_loop(1, CHIPS, wait_t2, 0)
    t2_local.wait()

    def new_copy(i):
        to = lax.rem(chip + i, CHIPS)
        return remote(
            new_s.at[to], new_out.at[mine], new_ss.at[i], new_rs.at[mine], to * 2 + core, exp
        )

    sq_s[...] = jnp.zeros_like(sq_s)
    cots = cot_r[...].reshape(REP * TOKENS, HIDDEN)

    def gradient(i):
        at = lax.rem(chip + i, CHIPS)
        columns = pl.ds(pl.multiple_of(at * SHARD, SHARD), SHARD)
        feats = t2_r[:, :, columns].reshape(REP * TOKENS, SHARD)
        grad = dot_rows(feats, cots)
        mom = decay_rate * mom_r[at].astype(f32) + grad
        new_s[at] = mom.astype(bf16)
        nest = (grad + decay_rate * mom).astype(bf16)
        nest_s[at] = nest
        wide = nest.astype(f32)
        squares = jnp.sum((wide * wide).reshape(SHARD // 8, 8, HIDDEN // 128, 128), axis=(0, 2))
        sq_s[...] += squares

    def gradient_send(i, carry):
        wait_mom(lax.rem(chip + i, CHIPS))
        gradient(i)
        new_copy(i).start()
        return carry

    lax.fori_loop(1, CHIPS, gradient_send, 0)
    mom_local.wait()
    gradient(0)
    new_local = pltpu.make_async_copy(new_s.at[chip], new_out.at[mine], local_sem.at[4])
    new_local.start()

    def gram_tile(j, carry):
        columns = pl.ds(pl.multiple_of(j * TILE, TILE), TILE)
        values = nest_s[...].reshape(CHIPS * SHARD, HIDDEN)
        tile = dot_rows(values, nest_s[:, :, columns].reshape(CHIPS * SHARD, TILE))
        gram_f[:, columns] = tile
        gram_s[:, columns] = tile.astype(bf16)
        return carry

    lax.fori_loop(0, HIDDEN // TILE, gram_tile, 0)
    swap_gram = remote(gram_s, gram_r, pair_ss.at[0], pair_rs.at[0], rep_core, exp)
    swap_sq = remote(sq_s, sq_r, pair_ss.at[1], pair_rs.at[1], rep_core, exp)
    swap_gram.start()
    swap_sq.start()
    swap_sq.wait()
    swap_gram.wait()

    total = jnp.sum(jnp.sum(sq_s[...] + sq_r[...], axis=0, keepdims=True), axis=1, keepdims=True)
    inverse = 1.0 / (jnp.sqrt(total) + norm_eps)
    g0[...] = ((gram_f[...] + gram_r[...].astype(f32)) * inverse * inverse).astype(bf16)

    def tiles(body):
        def one(j, carry):
            body(pl.ds(pl.multiple_of(j * TILE, TILE), TILE))
            return carry

        lax.fori_loop(0, HIDDEN // TILE, one, 0)

    def bend0_tile(at):
        bend0[:, at] = (
            coef_b * g0[:, at].astype(f32) + coef_c * dot32(g0[...], g0[:, at])
        ).astype(bf16)

    def step_tile(at):
        step[:, at] = (
            coef_a * g0[:, at].astype(f32) + dot32(g0[...], bend0[:, at])
        ).astype(bf16)

    def g1_tile(at):
        g1[:, at] = (
            coef_a * step[:, at].astype(f32) + dot32(bend0[...], step[:, at])
        ).astype(bf16)

    def bend1_tile(at):
        bend1[:, at] = (
            coef_b * g1[:, at].astype(f32) + coef_c * dot32(g1[...], g1[:, at])
        ).astype(bf16)

    def both_tile(at):
        both[:, at] = (
            coef_a * (bend0[:, at].astype(f32) + bend1[:, at].astype(f32))
            + dot32(bend0[...], bend1[:, at])
        ).astype(bf16)

    for body in (bend0_tile, step_tile, g1_tile, bend1_tile, both_tile):
        tiles(body)

    scale = math.sqrt(WIDTH) * inverse

    def upd_copy(i):
        to = lax.rem(chip + i, CHIPS)
        return remote(
            upd_s.at[to], upd_out.at[mine], upd_ss.at[i], upd_rs.at[mine], to * 2 + core, exp
        )

    def turn(i):
        at = lax.rem(chip + i, CHIPS)
        rows = nest_s[at]
        turned = coef_a * coef_a * rows.astype(f32) + dot32(rows, both[...])
        upd_s[at] = (turned * scale).astype(bf16)

    def turn_send(i, carry):
        turn(i)
        upd_copy(i).start()
        return carry

    lax.fori_loop(1, CHIPS, turn_send, 0)
    turn(0)
    upd_local = pltpu.make_async_copy(upd_s.at[chip], upd_out.at[mine], local_sem.at[5])
    upd_local.start()

    def wait_new(i, carry):
        source = lax.rem(chip + i, CHIPS)
        remote(
            new_s.at[0],
            new_out.at[matrix(source)],
            new_ss.at[i],
            new_rs.at[matrix(source)],
            source * 2 + core,
            exp,
        ).wait_recv()
        return carry

    lax.fori_loop(1, CHIPS, wait_new, 0)
    new_local.wait()

    mix = jnp.where(
        out_row == lax.rem(in_row, SHARD // 2) * 2 + in_row // (SHARD // 2), 1.0, 0.0
    ).astype(bf16)

    def interleave(source, target, expert):
        for part in range(2):
            half = slice(part * (SHARD // 2), (part + 1) * (SHARD // 2))
            pair = jnp.concatenate(
                [source[2 * expert, half], source[2 * expert + 1, half]], axis=0
            )
            target[half, expert] = (
                dot32(mix, pair).astype(bf16).reshape(SHARD // 2, 2, HIDDEN)
            )

    for expert in range(EXPERTS_HERE):
        interleave(new_out, new_mix, expert)

    tok_copy(0, 1).wait_send()

    def finish_tok(i, carry):
        tok_copy(i, 0).wait_send()
        tok_copy(i, 1).wait_send()
        return carry

    lax.fori_loop(1, EXP, finish_tok, 0)

    forward(chip).wait_send()
    for i in range(7):
        mom_copy(i).wait_send()

    def finish(i, carry):
        cot_copy(i).wait_send()
        forward(lax.rem(chip + i, CHIPS)).wait_send()
        t2_copy(i).wait_send()
        new_copy(i).wait_send()
        return carry

    lax.fori_loop(1, CHIPS, finish, 0)
    def collect(i, carry):
        side = lax.rem(x + i // 2, 2)
        half = lax.rem(y // 2 + i, 2)
        for kind in range(2):
            source = 2 * (2 * half + kind) + side

            @pl.when(source == chip)
            def _():
                upd_local.wait()

            @pl.when(source != chip)
            def _():
                remote(
                    upd_s.at[0],
                    upd_out.at[matrix(source)],
                    upd_ss.at[0],
                    upd_rs.at[matrix(source)],
                    source * 2 + core,
                    exp,
                ).wait_recv()

        interleave(upd_out, upd_mix, 2 * side + half)
        return carry

    lax.fori_loop(0, EXPERTS_HERE, collect, 0)

    def finish_upd(i, carry):
        upd_copy(i).wait_send()
        return carry

    lax.fori_loop(1, CHIPS, finish_upd, 0)


def on_device(acts, cotangent, counts, momentum):
    live = counts.reshape(EXP * EXPERTS_HERE)
    tok = acts.reshape(EXP * EXPERTS_HERE, SLOTS, WIDTH)
    cot = cotangent.reshape(CHIPS, TOKENS, HIDDEN)
    vmem = pltpu.VMEM
    dma = pltpu.SemaphoreType.DMA
    square = (HIDDEN, HIDDEN)
    rows = (CHIPS, SHARD, HIDDEN)
    mixed = (SHARD, EXPERTS_HERE, 2, HIDDEN)
    return pl.pallas_call(
        kernel,
        out_shape=(pltpu.VMEM(mixed, bf16),) * 2,
        in_specs=[
            pl.BlockSpec(memory_space=pltpu.SMEM),
            pl.BlockSpec(memory_space=pl.ANY),
            pl.BlockSpec(memory_space=pl.ANY),
            pl.BlockSpec(memory_space=pl.ANY),
        ],
        out_specs=(pl.BlockSpec(memory_space=pltpu.VMEM),) * 2,
        scratch_shapes=[
            vmem((EXP * EXPERTS_HERE, SLOTS, WIDTH), bf16),
            vmem(mixed, bf16),
            vmem(rows, bf16),
            vmem(rows, bf16),
            vmem(rows, bf16),
            vmem((EXP, SIDES, SIDE_ROWS, WIDTH), bf16),
            vmem((SIDES, EXP, SIDE_ROWS, WIDTH), bf16),
            vmem((SIDE_EXPERTS, 2, SIDES * TOKENS, HALF), bf16),
            vmem((CHIPS, 2 * TOKENS, HALF), bf16),
            vmem((CHIPS, 2, TOKENS, HIDDEN), bf16),
            vmem(rows, bf16),
            vmem(rows, bf16),
            vmem(rows, bf16),
            vmem(rows, bf16),
            vmem(square, bf16),
            vmem(square, bf16),
            vmem(square, f32),
            vmem((8, 128), f32),
            vmem((8, 128), f32),
            vmem(square, bf16),
            vmem(square, bf16),
            vmem(square, bf16),
            vmem(square, bf16),
            vmem(square, bf16),
            vmem(square, bf16),
            dma((2, EXP)),
            dma((2, EXP)),
            dma((CHIPS,)),
            dma((CHIPS, SIDES)),
            dma((CHIPS,)),
            dma((CHIPS,)),
            dma((CHIPS,)),
            dma((CHIPS,)),
            dma((CHIPS,)),
            dma((CHIPS,)),
            dma((CHIPS,)),
            dma((CHIPS,)),
            dma((CHIPS,)),
            dma((2,)),
            dma((2,)),
            dma((8,)),
            pltpu.SemaphoreType.REGULAR,
            pltpu.SemaphoreType.REGULAR,
        ],
        compiler_params=pltpu.CompilerParams(
            collective_id=0, has_side_effects=True, vmem_limit_bytes=60 << 20
        ),
        name="muon_owner",
    )(live, tok, cot, momentum)


def solution(mesh):
    in_specs = (
        P("rep", "exp", None, None, None),
        P("rep", "exp", None, None, None),
        P("rep", "exp", None),
        P("rep", "exp", None, None),
    )
    out_specs = (P("rep", "exp", None, None), P("rep", "exp", None, None))
    return jax.shard_map(
        on_device, mesh=mesh, in_specs=in_specs, out_specs=out_specs, check_vma=False
    )
```

```python
import functools
import math

import jax
import jax.numpy as jnp
from jax import lax
from jax.experimental import pallas as pl
from jax.experimental.pallas import tpu as pltpu
from jax.sharding import PartitionSpec as P

coef_a = 3.4445
coef_b = -4.775
coef_c = 2.0315
decay_rate = 0.95
norm_eps = 1e-07

REP = 16
EXP = 16
CHIPS = 8
YS = 4
EXPERTS_HERE = 4
SIDES = 2
SIDE_EXPERTS = EXPERTS_HERE // SIDES
SLOTS = 2
SIDE_ROWS = SIDE_EXPERTS * SLOTS
WIDTH = 2048
HALF = WIDTH // 2
SHARD = 128
HIDDEN = 768
TOKENS = 32
TILE = 256
EARLY = 4
LEADER = 0
MESSENGER = 1

MESH = pl.DeviceIdType.MESH
f32 = jnp.float32
bf16 = jnp.bfloat16


def remote(src, dst, send_sem, recv_sem, rep, exp):
    return pltpu.make_async_remote_copy(
        src_ref=src,
        dst_ref=dst,
        send_sem=send_sem,
        recv_sem=recv_sem,
        device_id=(rep, exp),
        device_id_type=MESH,
    )


def dot32(left, right):
    return jnp.dot(left, right, preferred_element_type=f32)


def dot_rows(left, right):
    return lax.dot_general(left, right, (((0,), (0,)), ((), ())), preferred_element_type=f32)


def kernel(
    counts,
    acts_hbm,
    cot_in,
    mom_hbm,
    new_mix,
    upd_mix,
    acts_in,
    mom_raw,
    mom_in,
    new_out,
    upd_out,
    tok_in,
    tok_r,
    t2_s,
    t2_r,
    cot_r,
    mom_r,
    new_s,
    nest_s,
    upd_s,
    gram_s,
    gram_r,
    gram_f,
    sq_s,
    sq_r,
    g0,
    bend0,
    step,
    g1,
    bend1,
    both,
    tok_ss,
    tok_rs,
    cot_ss,
    cot_rs,
    fwd_ss,
    mom_ss,
    mom_rs,
    t2_ss,
    t2_rs,
    new_ss,
    new_rs,
    upd_ss,
    upd_rs,
    pair_ss,
    pair_rs,
    local_sem,
    group_sem,
    all_sem,
):
    rep = lax.axis_index("rep")
    exp = lax.axis_index("exp")
    chip = rep // 2
    core = lax.rem(rep, 2)
    y = rep // 4
    x = lax.rem(chip, 2)
    peer = y * 2 + core
    rep_x = y * 4 + (1 - x) * 2 + core
    rep_core = chip * 2 + (1 - core)
    mine = 4 * x + y

    def matrix(of_chip):
        return 4 * lax.rem(of_chip, 2) + of_chip // 2

    def signal(to_rep, to_exp):
        pl.semaphore_signal(
            pltpu.get_barrier_semaphore(), inc=1, device_id=(to_rep, to_exp), device_id_type=MESH
        )

    acts_load = pltpu.make_async_copy(acts_hbm, acts_in, local_sem.at[6])
    mom_load = pltpu.make_async_copy(mom_hbm, mom_raw, local_sem.at[7])
    acts_load.start()
    mom_load.start()

    @pl.when(rep != LEADER)
    def _():
        signal(LEADER, exp)

    near = jnp.where(rep == LEADER, MESSENGER, rep)
    cross = jnp.where(rep_x == LEADER, MESSENGER, rep_x)

    def greet(i, carry):
        to = lax.rem(exp + i, EXP)
        signal(near, to)
        signal(cross, to)
        return carry

    @pl.when(rep_x != LEADER)
    def _():
        signal(rep_x, exp)

    lax.fori_loop(1, EXP, greet, 0)

    @pl.when(rep == LEADER)
    def _():
        pl.semaphore_wait(pltpu.get_barrier_semaphore(), REP - 1)

        def tell(i, carry):
            pl.semaphore_signal(
                group_sem, inc=1, device_id=(lax.rem(rep + i, REP), exp), device_id_type=MESH
            )
            return carry

        lax.fori_loop(1, REP, tell, 0)

    row = lax.broadcasted_iota(jnp.int32, (SIDE_ROWS, WIDTH), 0)

    def mask(i, carry):
        group = i // SIDES
        side = lax.rem(i, SIDES)
        at = i * SIDE_EXPERTS
        count = jnp.where(row < SLOTS, counts[at], counts[at + 1])
        values = acts_in[pl.ds(at, SIDE_EXPERTS)].astype(f32).reshape(SIDE_ROWS, WIDTH)
        tok_in[group, side] = jnp.where(lax.rem(row, SLOTS) < count, values, 0.0).astype(bf16)
        return carry

    acts_load.wait()
    lax.fori_loop(0, EXP * SIDES, mask, 0)
    def tok_copy(i, other):
        to = lax.rem(exp + i, EXP)
        return remote(
            tok_in.at[to, 1 - x if other else x],
            tok_r.at[x, exp],
            tok_ss.at[other, i],
            tok_rs.at[x, exp],
            rep_x if other else rep,
            to,
        )

    def cot_copy(i):
        to = lax.rem(chip + i, CHIPS)
        return remote(
            cot_in.at[matrix(to)],
            cot_r.at[peer, x],
            cot_ss.at[i],
            cot_rs.at[peer, x],
            to * 2 + core,
            exp,
        )

    def mom_copy(i):
        step, turned = (i, 1 - x) if i < YS else (i - YS + 1, x)
        to = 2 * lax.rem(y + step, YS) + turned
        return remote(
            mom_in.at[matrix(to)],
            mom_r.at[chip],
            mom_ss.at[i],
            mom_rs.at[chip],
            to * 2 + core,
            exp,
        )

    tok_local = pltpu.make_async_copy(tok_in.at[exp, x], tok_r.at[x, exp], local_sem.at[0])
    cot_local = pltpu.make_async_copy(cot_in.at[mine], cot_r.at[peer, x], local_sem.at[1])
    mom_local = pltpu.make_async_copy(mom_in.at[mine], mom_r.at[chip], local_sem.at[2])

    def start_cot(i, carry):
        cot_copy(i).start()
        return carry

    def hear_group(listens):
        @pl.when(listens)
        def _():
            pl.semaphore_wait(group_sem, 1)

        lax.fori_loop(1, CHIPS, start_cot, 0)

    def split_momentum():
        mom_load.wait()
        for expert in range(EXPERTS_HERE):
            mom_in[2 * expert : 2 * expert + 2] = jnp.swapaxes(mom_raw[:, expert], 0, 1)

    early = exp // 2 < EARLY

    @pl.when(early)
    def _():
        split_momentum()
        hear_group(rep != LEADER)
        for i in range(4, 7):
            mom_copy(i).start()

    @pl.when(rep == LEADER)
    def _():
        pl.semaphore_wait(all_sem, 1)

    @pl.when(jnp.logical_and(rep == MESSENGER, jnp.logical_not(early)))
    def _():
        pl.semaphore_wait(group_sem, 1)

    @pl.when(rep == MESSENGER)
    def _():
        pl.semaphore_wait(pltpu.get_barrier_semaphore(), 4 * (EXP - 1) + 1)
        pl.semaphore_signal(all_sem, inc=1, device_id=(LEADER, exp), device_id_type=MESH)

    @pl.when(jnp.logical_and(rep != LEADER, rep != MESSENGER))
    def _():
        pl.semaphore_wait(pltpu.get_barrier_semaphore(), 2 * (EXP - 1) + 1)

    tok_copy(0, 1).start()

    def start_tok(i, carry):
        tok_copy(i, 0).start()
        tok_copy(i, 1).start()
        return carry

    lax.fori_loop(1, EXP, start_tok, 0)

    @pl.when(jnp.logical_not(early))
    def _():
        hear_group(jnp.logical_and(rep != LEADER, rep != MESSENGER))
        split_momentum()
        for i in range(4, 7):
            mom_copy(i).start()

    for i in range(4):
        mom_copy(i).start()

    tok_local.start()
    cot_local.start()
    mom_local.start()

    out_row = lax.broadcasted_iota(jnp.int32, (SHARD, SHARD), 0)
    in_row = lax.broadcasted_iota(jnp.int32, (SHARD, SHARD), 1)
    wanted = (
        lax.rem(out_row // SLOTS, SIDES * EXP) * SIDE_ROWS
        + (out_row // (SIDES * TOKENS)) * SLOTS
        + lax.rem(out_row, SLOTS)
    )
    order = jnp.where(in_row == wanted, 1.0, 0.0).astype(bf16)

    def wait_tok(i, carry):
        source = lax.rem(exp + i, EXP)
        remote(
            tok_in.at[0, 0], tok_r.at[x, source], tok_ss.at[0, i], tok_rs.at[x, source], rep, source
        ).wait_recv()
        return carry

    lax.fori_loop(1, EXP, wait_tok, 0)

    def wait_tok_x(i, carry):
        source = lax.rem(exp + i, EXP)
        remote(
            tok_in.at[0, 0],
            tok_r.at[1 - x, source],
            tok_ss.at[1, i],
            tok_rs.at[1 - x, source],
            rep_x,
            source,
        ).wait_recv()
        return carry

    lax.fori_loop(0, EXP, wait_tok_x, 0)
    tok_local.wait()

    rows = tok_r[...].reshape(SIDES * EXP * SIDE_ROWS, WIDTH)
    for piece in range(REP):
        part = dot32(order, rows[:, piece * SHARD : (piece + 1) * SHARD]).astype(bf16)
        for expert in range(SIDE_EXPERTS):
            t2_s[expert, piece % 2, :, (piece // 2) * SHARD : (piece // 2 + 1) * SHARD] = part[
                expert * SIDES * TOKENS : (expert + 1) * SIDES * TOKENS
            ]

    def t2_copy(i):
        to = lax.rem(peer + i, CHIPS)
        return remote(
            t2_s.at[to // 4, lax.rem(to, 2)],
            t2_r.at[peer],
            t2_ss.at[i],
            t2_rs.at[peer],
            (to // 2) * 4 + x * 2 + lax.rem(to, 2),
            exp,
        )

    def start_t2(i, carry):
        t2_copy(i).start()
        return carry

    lax.fori_loop(1, CHIPS, start_t2, 0)
    t2_local = pltpu.make_async_copy(t2_s.at[y // 2, core], t2_r.at[peer], local_sem.at[3])
    t2_local.start()

    def forward(of_chip):
        at = (of_chip // 2) * 2 + core
        side = lax.rem(of_chip, 2)
        return remote(
            cot_r.at[at, side],
            cot_r.at[at, side],
            fwd_ss.at[of_chip],
            cot_rs.at[at, side],
            rep_core,
            exp,
        )

    def wait_cot(i, carry):
        source = lax.rem(chip + i, CHIPS)
        at = (source // 2) * 2 + core
        side = lax.rem(source, 2)
        remote(
            cot_in.at[0],
            cot_r.at[at, side],
            cot_ss.at[i],
            cot_rs.at[at, side],
            source * 2 + core,
            exp,
        ).wait_recv()
        forward(source).start()
        return carry

    cot_local.wait()
    forward(chip).start()
    lax.fori_loop(1, CHIPS, wait_cot, 0)

    def wait_forward(i, carry):
        at = (i // 2) * 2 + 1 - core
        side = lax.rem(i, 2)
        remote(
            cot_r.at[at, side],
            cot_r.at[at, side],
            fwd_ss.at[i],
            cot_rs.at[at, side],
            rep_core,
            exp,
        ).wait_recv()
        return carry

    lax.fori_loop(0, CHIPS, wait_forward, 0)

    def wait_mom(source):
        remote(
            mom_in.at[0],
            mom_r.at[source],
            mom_ss.at[0],
            mom_rs.at[source],
            source * 2 + core,
            exp,
        ).wait_recv()

    def wait_t2(i, carry):
        source = lax.rem(peer + i, CHIPS)
        remote(
            t2_s.at[0],
            t2_r.at[source],
            t2_ss.at[i],
            t2_rs.at[source],
            (source // 2) * 4 + x * 2 + lax.rem(source, 2),
            exp,
        ).wait_recv()
        return carry

    lax.fori_loop(1, CHIPS, wait_t2, 0)
    t2_local.wait()

    def new_copy(i):
        to = lax.rem(chip + i, CHIPS)
        return remote(
            new_s.at[to], new_out.at[mine], new_ss.at[i], new_rs.at[mine], to * 2 + core, exp
        )

    sq_s[...] = jnp.zeros_like(sq_s)
    cots = cot_r[...].reshape(REP * TOKENS, HIDDEN)

    def gradient(i, sent):
        at = lax.rem(chip + i, CHIPS)
        columns = pl.ds(pl.multiple_of(at * SHARD, SHARD), SHARD)
        feats = t2_r[:, :, columns].reshape(REP * TOKENS, SHARD)
        grad = dot_rows(feats, cots)
        mom = decay_rate * mom_r[at].astype(f32) + grad
        new_s[at] = mom.astype(bf16)
        sent(at)
        nest = (grad + decay_rate * mom).astype(bf16)
        nest_s[at] = nest

    def add_squares(at, carry):
        wide = nest_s[at].astype(f32)
        squares = jnp.sum((wide * wide).reshape(SHARD // 8, 8, HIDDEN // 128, 128), axis=(0, 2))
        sq_s[...] += squares
        return carry

    def gradient_send(i, carry):
        wait_mom(lax.rem(chip + i, CHIPS))
        gradient(i, lambda at: new_copy(i).start())
        return carry

    lax.fori_loop(1, CHIPS, gradient_send, 0)
    mom_local.wait()
    new_local = pltpu.make_async_copy(new_s.at[chip], new_out.at[mine], local_sem.at[4])
    gradient(0, lambda at: new_local.start())
    lax.fori_loop(0, CHIPS, add_squares, 0)

    def gram_tile(j, carry):
        columns = pl.ds(pl.multiple_of(j * TILE, TILE), TILE)
        values = nest_s[...].reshape(CHIPS * SHARD, HIDDEN)
        tile = dot_rows(values, nest_s[:, :, columns].reshape(CHIPS * SHARD, TILE))
        gram_f[:, columns] = tile
        gram_s[:, columns] = tile.astype(bf16)
        return carry

    lax.fori_loop(0, HIDDEN // TILE, gram_tile, 0)
    swap_gram = remote(gram_s, gram_r, pair_ss.at[0], pair_rs.at[0], rep_core, exp)
    swap_sq = remote(sq_s, sq_r, pair_ss.at[1], pair_rs.at[1], rep_core, exp)
    swap_gram.start()
    swap_sq.start()
    swap_sq.wait()
    swap_gram.wait()

    total = jnp.sum(jnp.sum(sq_s[...] + sq_r[...], axis=0, keepdims=True), axis=1, keepdims=True)
    inverse = 1.0 / (jnp.sqrt(total) + norm_eps)
    g0[...] = ((gram_f[...] + gram_r[...].astype(f32)) * inverse * inverse).astype(bf16)

    def tiles(body):
        def one(j, carry):
            body(pl.ds(pl.multiple_of(j * TILE, TILE), TILE))
            return carry

        lax.fori_loop(0, HIDDEN // TILE, one, 0)

    def bend0_tile(at):
        bend0[:, at] = (
            coef_b * g0[:, at].astype(f32) + coef_c * dot32(g0[...], g0[:, at])
        ).astype(bf16)

    def step_tile(at):
        step[:, at] = (
            coef_a * g0[:, at].astype(f32) + dot32(g0[...], bend0[:, at])
        ).astype(bf16)

    def g1_tile(at):
        g1[:, at] = (
            coef_a * step[:, at].astype(f32) + dot32(bend0[...], step[:, at])
        ).astype(bf16)

    def bend1_tile(at):
        bend1[:, at] = (
            coef_b * g1[:, at].astype(f32) + coef_c * dot32(g1[...], g1[:, at])
        ).astype(bf16)

    def both_tile(at):
        both[:, at] = (
            coef_a * (bend0[:, at].astype(f32) + bend1[:, at].astype(f32))
            + dot32(bend0[...], bend1[:, at])
        ).astype(bf16)

    for body in (bend0_tile, step_tile, g1_tile, bend1_tile, both_tile):
        tiles(body)

    scale = math.sqrt(WIDTH) * inverse

    def upd_copy(i):
        to = lax.rem(chip + i, CHIPS)
        return remote(
            upd_s.at[to], upd_out.at[mine], upd_ss.at[i], upd_rs.at[mine], to * 2 + core, exp
        )

    def turn(i):
        at = lax.rem(chip + i, CHIPS)
        rows = nest_s[at]
        turned = coef_a * coef_a * rows.astype(f32) + dot32(rows, both[...])
        upd_s[at] = (turned * scale).astype(bf16)

    def turn_send(i, carry):
        turn(i)
        upd_copy(i).start()
        return carry

    lax.fori_loop(1, CHIPS, turn_send, 0)
    turn(0)
    upd_local = pltpu.make_async_copy(upd_s.at[chip], upd_out.at[mine], local_sem.at[5])
    upd_local.start()

    def wait_new(i, carry):
        source = lax.rem(chip + i, CHIPS)
        remote(
            new_s.at[0],
            new_out.at[matrix(source)],
            new_ss.at[i],
            new_rs.at[matrix(source)],
            source * 2 + core,
            exp,
        ).wait_recv()
        return carry

    lax.fori_loop(1, CHIPS, wait_new, 0)
    new_local.wait()

    mix = jnp.where(
        out_row == lax.rem(in_row, SHARD // 2) * 2 + in_row // (SHARD // 2), 1.0, 0.0
    ).astype(bf16)

    def interleave(source, target, expert):
        for part in range(2):
            half = slice(part * (SHARD // 2), (part + 1) * (SHARD // 2))
            pair = jnp.concatenate(
                [source[2 * expert, half], source[2 * expert + 1, half]], axis=0
            )
            target[half, expert] = (
                dot32(mix, pair).astype(bf16).reshape(SHARD // 2, 2, HIDDEN)
            )

    for expert in range(EXPERTS_HERE):
        interleave(new_out, new_mix, expert)

    tok_copy(0, 1).wait_send()

    def finish_tok(i, carry):
        tok_copy(i, 0).wait_send()
        tok_copy(i, 1).wait_send()
        return carry

    lax.fori_loop(1, EXP, finish_tok, 0)

    forward(chip).wait_send()
    for i in range(7):
        mom_copy(i).wait_send()

    def finish(i, carry):
        cot_copy(i).wait_send()
        forward(lax.rem(chip + i, CHIPS)).wait_send()
        t2_copy(i).wait_send()
        new_copy(i).wait_send()
        return carry

    lax.fori_loop(1, CHIPS, finish, 0)
    def collect(i, carry):
        side = lax.rem(x + i // 2, 2)
        half = lax.rem(y // 2 + i, 2)
        for kind in range(2):
            source = 2 * (2 * half + kind) + side

            @pl.when(source == chip)
            def _():
                upd_local.wait()

            @pl.when(source != chip)
            def _():
                remote(
                    upd_s.at[0],
                    upd_out.at[matrix(source)],
                    upd_ss.at[0],
                    upd_rs.at[matrix(source)],
                    source * 2 + core,
                    exp,
                ).wait_recv()

        interleave(upd_out, upd_mix, 2 * side + half)
        return carry

    lax.fori_loop(0, EXPERTS_HERE, collect, 0)

    def finish_upd(i, carry):
        upd_copy(i).wait_send()
        return carry

    lax.fori_loop(1, CHIPS, finish_upd, 0)


def on_device(acts, cotangent, counts, momentum):
    live = counts.reshape(EXP * EXPERTS_HERE)
    tok = acts.reshape(EXP * EXPERTS_HERE, SLOTS, WIDTH)
    cot = cotangent.reshape(CHIPS, TOKENS, HIDDEN)
    vmem = pltpu.VMEM
    dma = pltpu.SemaphoreType.DMA
    square = (HIDDEN, HIDDEN)
    rows = (CHIPS, SHARD, HIDDEN)
    mixed = (SHARD, EXPERTS_HERE, 2, HIDDEN)
    return pl.pallas_call(
        kernel,
        out_shape=(pltpu.VMEM(mixed, bf16),) * 2,
        in_specs=[
            pl.BlockSpec(memory_space=pltpu.SMEM),
            pl.BlockSpec(memory_space=pl.ANY),
            pl.BlockSpec(memory_space=pl.ANY),
            pl.BlockSpec(memory_space=pl.ANY),
        ],
        out_specs=(pl.BlockSpec(memory_space=pltpu.VMEM),) * 2,
        scratch_shapes=[
            vmem((EXP * EXPERTS_HERE, SLOTS, WIDTH), bf16),
            vmem(mixed, bf16),
            vmem(rows, bf16),
            vmem(rows, bf16),
            vmem(rows, bf16),
            vmem((EXP, SIDES, SIDE_ROWS, WIDTH), bf16),
            vmem((SIDES, EXP, SIDE_ROWS, WIDTH), bf16),
            vmem((SIDE_EXPERTS, 2, SIDES * TOKENS, HALF), bf16),
            vmem((CHIPS, 2 * TOKENS, HALF), bf16),
            vmem((CHIPS, 2, TOKENS, HIDDEN), bf16),
            vmem(rows, bf16),
            vmem(rows, bf16),
            vmem(rows, bf16),
            vmem(rows, bf16),
            vmem(square, bf16),
            vmem(square, bf16),
            vmem(square, f32),
            vmem((8, 128), f32),
            vmem((8, 128), f32),
            vmem(square, bf16),
            vmem(square, bf16),
            vmem(square, bf16),
            vmem(square, bf16),
            vmem(square, bf16),
            vmem(square, bf16),
            dma((2, EXP)),
            dma((2, EXP)),
            dma((CHIPS,)),
            dma((CHIPS, SIDES)),
            dma((CHIPS,)),
            dma((CHIPS,)),
            dma((CHIPS,)),
            dma((CHIPS,)),
            dma((CHIPS,)),
            dma((CHIPS,)),
            dma((CHIPS,)),
            dma((CHIPS,)),
            dma((CHIPS,)),
            dma((2,)),
            dma((2,)),
            dma((8,)),
            pltpu.SemaphoreType.REGULAR,
            pltpu.SemaphoreType.REGULAR,
        ],
        compiler_params=pltpu.CompilerParams(
            collective_id=0, has_side_effects=True, vmem_limit_bytes=60 << 20
        ),
        name="muon_owner",
    )(live, tok, cot, momentum)


def solution(mesh):
    in_specs = (
        P("rep", "exp", None, None, None),
        P("rep", "exp", None, None, None),
        P("rep", "exp", None),
        P("rep", "exp", None, None),
    )
    out_specs = (P("rep", "exp", None, None), P("rep", "exp", None, None))
    return jax.shard_map(
        on_device, mesh=mesh, in_specs=in_specs, out_specs=out_specs, check_vma=False
    )
```

```python
import functools
import math

import jax
import jax.numpy as jnp
from jax import lax
from jax.experimental import pallas as pl
from jax.experimental.pallas import tpu as pltpu
from jax.sharding import PartitionSpec as P

coef_a = 3.4445
coef_b = -4.775
coef_c = 2.0315
decay_rate = 0.95
norm_eps = 1e-07

REP = 16
EXP = 16
CHIPS = 8
YS = 4
EXPERTS_HERE = 4
SIDES = 2
SIDE_EXPERTS = EXPERTS_HERE // SIDES
SLOTS = 2
SIDE_ROWS = SIDE_EXPERTS * SLOTS
WIDTH = 2048
HALF = WIDTH // 2
SHARD = 128
HIDDEN = 768
TOKENS = 32
TILE = 256
EARLY = 4
LEADER = 0
MESSENGER = 1

MESH = pl.DeviceIdType.MESH
f32 = jnp.float32
bf16 = jnp.bfloat16


def remote(src, dst, send_sem, recv_sem, rep, exp):
    return pltpu.make_async_remote_copy(
        src_ref=src,
        dst_ref=dst,
        send_sem=send_sem,
        recv_sem=recv_sem,
        device_id=(rep, exp),
        device_id_type=MESH,
    )


def dot32(left, right):
    return jnp.dot(left, right, preferred_element_type=f32)


def dot_rows(left, right):
    return lax.dot_general(left, right, (((0,), (0,)), ((), ())), preferred_element_type=f32)


def kernel(
    counts,
    acts_hbm,
    cot_in,
    mom_hbm,
    new_mix,
    upd_mix,
    acts_in,
    mom_raw,
    mom_in,
    new_out,
    upd_out,
    tok_in,
    tok_r,
    t2_s,
    t2_r,
    cot_r,
    mom_r,
    new_s,
    nest_s,
    upd_s,
    gram_s,
    gram_r,
    gram_f,
    sq_s,
    sq_r,
    g0,
    bend0,
    step,
    g1,
    bend1,
    both,
    tok_ss,
    tok_rs,
    cot_ss,
    cot_rs,
    fwd_ss,
    mom_ss,
    mom_rs,
    t2_ss,
    t2_rs,
    new_ss,
    new_rs,
    upd_ss,
    upd_rs,
    pair_ss,
    pair_rs,
    local_sem,
    group_sem,
    all_sem,
):
    rep = lax.axis_index("rep")
    exp = lax.axis_index("exp")
    chip = rep // 2
    core = lax.rem(rep, 2)
    y = rep // 4
    x = lax.rem(chip, 2)
    peer = y * 2 + core
    rep_x = y * 4 + (1 - x) * 2 + core
    rep_core = chip * 2 + (1 - core)
    mine = 4 * x + y

    def matrix(of_chip):
        return 4 * lax.rem(of_chip, 2) + of_chip // 2

    def signal(to_rep, to_exp):
        pl.semaphore_signal(
            pltpu.get_barrier_semaphore(), inc=1, device_id=(to_rep, to_exp), device_id_type=MESH
        )

    acts_load = pltpu.make_async_copy(acts_hbm, acts_in, local_sem.at[6])
    mom_load = pltpu.make_async_copy(mom_hbm, mom_raw, local_sem.at[7])
    acts_load.start()
    mom_load.start()

    @pl.when(rep != LEADER)
    def _():
        signal(LEADER, exp)

    near = jnp.where(rep == LEADER, MESSENGER, rep)
    cross = jnp.where(rep_x == LEADER, MESSENGER, rep_x)

    def greet(i, carry):
        to = lax.rem(exp + i, EXP)
        signal(near, to)
        signal(cross, to)
        return carry

    @pl.when(rep_x != LEADER)
    def _():
        signal(rep_x, exp)

    lax.fori_loop(1, EXP, greet, 0)

    @pl.when(rep == LEADER)
    def _():
        pl.semaphore_wait(pltpu.get_barrier_semaphore(), REP - 1)

        def tell(i, carry):
            pl.semaphore_signal(
                group_sem, inc=1, device_id=(lax.rem(rep + i, REP), exp), device_id_type=MESH
            )
            return carry

        lax.fori_loop(1, REP, tell, 0)

    row = lax.broadcasted_iota(jnp.int32, (SIDE_ROWS, WIDTH), 0)

    def mask(i, carry):
        group = i // SIDES
        side = lax.rem(i, SIDES)
        at = i * SIDE_EXPERTS
        count = jnp.where(row < SLOTS, counts[at], counts[at + 1])
        values = acts_in[pl.ds(at, SIDE_EXPERTS)].astype(f32).reshape(SIDE_ROWS, WIDTH)
        tok_in[group, side] = jnp.where(lax.rem(row, SLOTS) < count, values, 0.0).astype(bf16)
        return carry

    acts_load.wait()
    lax.fori_loop(0, EXP * SIDES, mask, 0)
    def tok_copy(i, other):
        to = lax.rem(exp + i, EXP)
        return remote(
            tok_in.at[to, 1 - x if other else x],
            tok_r.at[x, exp],
            tok_ss.at[other, i],
            tok_rs.at[x, exp],
            rep_x if other else rep,
            to,
        )

    def cot_copy(i):
        to = lax.rem(chip + i, CHIPS)
        return remote(
            cot_in.at[matrix(to)],
            cot_r.at[peer, x],
            cot_ss.at[i],
            cot_rs.at[peer, x],
            to * 2 + core,
            exp,
        )

    def mom_copy(i):
        step, turned = (i, 1 - x) if i < YS else (i - YS + 1, x)
        to = 2 * lax.rem(y + step, YS) + turned
        return remote(
            mom_in.at[matrix(to)],
            mom_r.at[chip],
            mom_ss.at[i],
            mom_rs.at[chip],
            to * 2 + core,
            exp,
        )

    tok_local = pltpu.make_async_copy(tok_in.at[exp, x], tok_r.at[x, exp], local_sem.at[0])
    cot_local = pltpu.make_async_copy(cot_in.at[mine], cot_r.at[peer, x], local_sem.at[1])
    mom_local = pltpu.make_async_copy(mom_in.at[mine], mom_r.at[chip], local_sem.at[2])

    def start_cot(i, carry):
        cot_copy(i).start()
        return carry

    def hear_group(listens):
        @pl.when(listens)
        def _():
            pl.semaphore_wait(group_sem, 1)

        lax.fori_loop(1, CHIPS, start_cot, 0)

    def split_momentum():
        mom_load.wait()
        for expert in range(EXPERTS_HERE):
            mom_in[2 * expert : 2 * expert + 2] = jnp.swapaxes(mom_raw[:, expert], 0, 1)

    early = exp // 2 < EARLY

    @pl.when(early)
    def _():
        split_momentum()
        hear_group(rep != LEADER)
        for i in range(4, 7):
            mom_copy(i).start()

    @pl.when(rep == LEADER)
    def _():
        pl.semaphore_wait(all_sem, 1)

    @pl.when(jnp.logical_and(rep == MESSENGER, jnp.logical_not(early)))
    def _():
        pl.semaphore_wait(group_sem, 1)

    @pl.when(rep == MESSENGER)
    def _():
        pl.semaphore_wait(pltpu.get_barrier_semaphore(), 4 * (EXP - 1) + 1)
        pl.semaphore_signal(all_sem, inc=1, device_id=(LEADER, exp), device_id_type=MESH)

    @pl.when(jnp.logical_and(rep != LEADER, rep != MESSENGER))
    def _():
        pl.semaphore_wait(pltpu.get_barrier_semaphore(), 2 * (EXP - 1) + 1)

    tok_copy(0, 1).start()

    def start_tok(i, carry):
        tok_copy(i, 0).start()
        tok_copy(i, 1).start()
        return carry

    lax.fori_loop(1, EXP, start_tok, 0)

    @pl.when(jnp.logical_not(early))
    def _():
        hear_group(jnp.logical_and(rep != LEADER, rep != MESSENGER))
        split_momentum()
        for i in range(4, 7):
            mom_copy(i).start()

    for i in range(4):
        mom_copy(i).start()

    tok_local.start()
    cot_local.start()
    mom_local.start()

    out_row = lax.broadcasted_iota(jnp.int32, (SHARD, SHARD), 0)
    in_row = lax.broadcasted_iota(jnp.int32, (SHARD, SHARD), 1)
    wanted = (
        lax.rem(out_row // SLOTS, SIDES * EXP) * SIDE_ROWS
        + (out_row // (SIDES * TOKENS)) * SLOTS
        + lax.rem(out_row, SLOTS)
    )
    order = jnp.where(in_row == wanted, 1.0, 0.0).astype(bf16)

    def wait_tok(i, carry):
        source = lax.rem(exp + i, EXP)
        remote(
            tok_in.at[0, 0], tok_r.at[x, source], tok_ss.at[0, i], tok_rs.at[x, source], rep, source
        ).wait_recv()
        return carry

    lax.fori_loop(1, EXP, wait_tok, 0)

    def wait_tok_x(i, carry):
        source = lax.rem(exp + i, EXP)
        remote(
            tok_in.at[0, 0],
            tok_r.at[1 - x, source],
            tok_ss.at[1, i],
            tok_rs.at[1 - x, source],
            rep_x,
            source,
        ).wait_recv()
        return carry

    lax.fori_loop(0, EXP, wait_tok_x, 0)
    tok_local.wait()

    rows = tok_r[...].reshape(SIDES * EXP * SIDE_ROWS, WIDTH)
    for piece in range(REP):
        part = dot32(order, rows[:, piece * SHARD : (piece + 1) * SHARD]).astype(bf16)
        for expert in range(SIDE_EXPERTS):
            t2_s[expert, piece % 2, :, (piece // 2) * SHARD : (piece // 2 + 1) * SHARD] = part[
                expert * SIDES * TOKENS : (expert + 1) * SIDES * TOKENS
            ]

    def t2_copy(i):
        to = lax.rem(peer + i, CHIPS)
        return remote(
            t2_s.at[to // 4, lax.rem(to, 2)],
            t2_r.at[peer],
            t2_ss.at[i],
            t2_rs.at[peer],
            (to // 2) * 4 + x * 2 + lax.rem(to, 2),
            exp,
        )

    def start_t2(i, carry):
        t2_copy(i).start()
        return carry

    lax.fori_loop(1, CHIPS, start_t2, 0)
    t2_local = pltpu.make_async_copy(t2_s.at[y // 2, core], t2_r.at[peer], local_sem.at[3])
    t2_local.start()

    def forward(of_chip):
        at = (of_chip // 2) * 2 + core
        side = lax.rem(of_chip, 2)
        return remote(
            cot_r.at[at, side],
            cot_r.at[at, side],
            fwd_ss.at[of_chip],
            cot_rs.at[at, side],
            rep_core,
            exp,
        )

    def wait_cot(i, carry):
        source = lax.rem(chip + i, CHIPS)
        at = (source // 2) * 2 + core
        side = lax.rem(source, 2)
        remote(
            cot_in.at[0],
            cot_r.at[at, side],
            cot_ss.at[i],
            cot_rs.at[at, side],
            source * 2 + core,
            exp,
        ).wait_recv()
        forward(source).start()
        return carry

    cot_local.wait()
    forward(chip).start()
    lax.fori_loop(1, CHIPS, wait_cot, 0)

    def wait_forward(i, carry):
        at = (i // 2) * 2 + 1 - core
        side = lax.rem(i, 2)
        remote(
            cot_r.at[at, side],
            cot_r.at[at, side],
            fwd_ss.at[i],
            cot_rs.at[at, side],
            rep_core,
            exp,
        ).wait_recv()
        return carry

    lax.fori_loop(0, CHIPS, wait_forward, 0)

    def wait_mom(source):
        remote(
            mom_in.at[0],
            mom_r.at[source],
            mom_ss.at[0],
            mom_rs.at[source],
            source * 2 + core,
            exp,
        ).wait_recv()

    def wait_t2(i, carry):
        source = lax.rem(peer + i, CHIPS)
        remote(
            t2_s.at[0],
            t2_r.at[source],
            t2_ss.at[i],
            t2_rs.at[source],
            (source // 2) * 4 + x * 2 + lax.rem(source, 2),
            exp,
        ).wait_recv()
        return carry

    lax.fori_loop(1, CHIPS, wait_t2, 0)
    t2_local.wait()

    def turn_of(i):
        step = jnp.where(i < YS, i, i - YS)
        return 2 * lax.rem(y + step, YS) + jnp.where(i < YS, x, 1 - x)

    def new_copy(i):
        to = turn_of(i)
        return remote(
            new_s.at[to], new_out.at[mine], new_ss.at[i], new_rs.at[mine], to * 2 + core, exp
        )

    sq_s[...] = jnp.zeros_like(sq_s)
    cots = cot_r[...].reshape(REP * TOKENS, HIDDEN)

    def gradient(i):
        at = turn_of(i)
        columns = pl.ds(pl.multiple_of(at * SHARD, SHARD), SHARD)
        feats = t2_r[:, :, columns].reshape(REP * TOKENS, SHARD)
        grad = dot_rows(feats, cots)
        mom = decay_rate * mom_r[at].astype(f32) + grad
        new_s[at] = mom.astype(bf16)
        nest = (grad + decay_rate * mom).astype(bf16)
        nest_s[at] = nest
        wide = nest.astype(f32)
        squares = jnp.sum((wide * wide).reshape(SHARD // 8, 8, HIDDEN // 128, 128), axis=(0, 2))
        sq_s[...] += squares

    def gradient_send(i, carry):
        wait_mom(turn_of(i))
        gradient(i)
        new_copy(i).start()
        return carry

    lax.fori_loop(1, CHIPS, gradient_send, 0)
    mom_local.wait()
    gradient(0)
    new_local = pltpu.make_async_copy(new_s.at[chip], new_out.at[mine], local_sem.at[4])
    new_local.start()

    def gram_tile(j, carry):
        columns = pl.ds(pl.multiple_of(j * TILE, TILE), TILE)
        values = nest_s[...].reshape(CHIPS * SHARD, HIDDEN)
        tile = dot_rows(values, nest_s[:, :, columns].reshape(CHIPS * SHARD, TILE))
        gram_f[:, columns] = tile
        gram_s[:, columns] = tile.astype(bf16)
        return carry

    lax.fori_loop(0, HIDDEN // TILE, gram_tile, 0)
    swap_gram = remote(gram_s, gram_r, pair_ss.at[0], pair_rs.at[0], rep_core, exp)
    swap_sq = remote(sq_s, sq_r, pair_ss.at[1], pair_rs.at[1], rep_core, exp)
    swap_gram.start()
    swap_sq.start()
    swap_sq.wait()
    swap_gram.wait()

    total = jnp.sum(jnp.sum(sq_s[...] + sq_r[...], axis=0, keepdims=True), axis=1, keepdims=True)
    inverse = 1.0 / (jnp.sqrt(total) + norm_eps)
    g0[...] = ((gram_f[...] + gram_r[...].astype(f32)) * inverse * inverse).astype(bf16)

    def tiles(body):
        def one(j, carry):
            body(pl.ds(pl.multiple_of(j * TILE, TILE), TILE))
            return carry

        lax.fori_loop(0, HIDDEN // TILE, one, 0)

    def bend0_tile(at):
        bend0[:, at] = (
            coef_b * g0[:, at].astype(f32) + coef_c * dot32(g0[...], g0[:, at])
        ).astype(bf16)

    def step_tile(at):
        step[:, at] = (
            coef_a * g0[:, at].astype(f32) + dot32(g0[...], bend0[:, at])
        ).astype(bf16)

    def g1_tile(at):
        g1[:, at] = (
            coef_a * step[:, at].astype(f32) + dot32(bend0[...], step[:, at])
        ).astype(bf16)

    def bend1_tile(at):
        bend1[:, at] = (
            coef_b * g1[:, at].astype(f32) + coef_c * dot32(g1[...], g1[:, at])
        ).astype(bf16)

    def both_tile(at):
        both[:, at] = (
            coef_a * (bend0[:, at].astype(f32) + bend1[:, at].astype(f32))
            + dot32(bend0[...], bend1[:, at])
        ).astype(bf16)

    for body in (bend0_tile, step_tile, g1_tile, bend1_tile, both_tile):
        tiles(body)

    scale = math.sqrt(WIDTH) * inverse

    def upd_copy(i):
        to = lax.rem(chip + i, CHIPS)
        return remote(
            upd_s.at[to], upd_out.at[mine], upd_ss.at[i], upd_rs.at[mine], to * 2 + core, exp
        )

    def turn(i):
        at = lax.rem(chip + i, CHIPS)
        rows = nest_s[at]
        turned = coef_a * coef_a * rows.astype(f32) + dot32(rows, both[...])
        upd_s[at] = (turned * scale).astype(bf16)

    def turn_send(i, carry):
        turn(i)
        upd_copy(i).start()
        return carry

    lax.fori_loop(1, CHIPS, turn_send, 0)
    turn(0)
    upd_local = pltpu.make_async_copy(upd_s.at[chip], upd_out.at[mine], local_sem.at[5])
    upd_local.start()

    def wait_new(i, carry):
        source = lax.rem(chip + i, CHIPS)
        remote(
            new_s.at[0],
            new_out.at[matrix(source)],
            new_ss.at[i],
            new_rs.at[matrix(source)],
            source * 2 + core,
            exp,
        ).wait_recv()
        return carry

    lax.fori_loop(1, CHIPS, wait_new, 0)
    new_local.wait()

    mix = jnp.where(
        out_row == lax.rem(in_row, SHARD // 2) * 2 + in_row // (SHARD // 2), 1.0, 0.0
    ).astype(bf16)

    def interleave(source, target, expert):
        for part in range(2):
            half = slice(part * (SHARD // 2), (part + 1) * (SHARD // 2))
            pair = jnp.concatenate(
                [source[2 * expert, half], source[2 * expert + 1, half]], axis=0
            )
            target[half, expert] = (
                dot32(mix, pair).astype(bf16).reshape(SHARD // 2, 2, HIDDEN)
            )

    for expert in range(EXPERTS_HERE):
        interleave(new_out, new_mix, expert)

    tok_copy(0, 1).wait_send()

    def finish_tok(i, carry):
        tok_copy(i, 0).wait_send()
        tok_copy(i, 1).wait_send()
        return carry

    lax.fori_loop(1, EXP, finish_tok, 0)

    forward(chip).wait_send()
    for i in range(7):
        mom_copy(i).wait_send()

    def finish(i, carry):
        cot_copy(i).wait_send()
        forward(lax.rem(chip + i, CHIPS)).wait_send()
        t2_copy(i).wait_send()
        new_copy(i).wait_send()
        return carry

    lax.fori_loop(1, CHIPS, finish, 0)
    def collect(i, carry):
        side = lax.rem(x + i // 2, 2)
        half = lax.rem(y // 2 + i, 2)
        for kind in range(2):
            source = 2 * (2 * half + kind) + side

            @pl.when(source == chip)
            def _():
                upd_local.wait()

            @pl.when(source != chip)
            def _():
                remote(
                    upd_s.at[0],
                    upd_out.at[matrix(source)],
                    upd_ss.at[0],
                    upd_rs.at[matrix(source)],
                    source * 2 + core,
                    exp,
                ).wait_recv()

        interleave(upd_out, upd_mix, 2 * side + half)
        return carry

    lax.fori_loop(0, EXPERTS_HERE, collect, 0)

    def finish_upd(i, carry):
        upd_copy(i).wait_send()
        return carry

    lax.fori_loop(1, CHIPS, finish_upd, 0)


def on_device(acts, cotangent, counts, momentum):
    live = counts.reshape(EXP * EXPERTS_HERE)
    tok = acts.reshape(EXP * EXPERTS_HERE, SLOTS, WIDTH)
    cot = cotangent.reshape(CHIPS, TOKENS, HIDDEN)
    vmem = pltpu.VMEM
    dma = pltpu.SemaphoreType.DMA
    square = (HIDDEN, HIDDEN)
    rows = (CHIPS, SHARD, HIDDEN)
    mixed = (SHARD, EXPERTS_HERE, 2, HIDDEN)
    return pl.pallas_call(
        kernel,
        out_shape=(pltpu.VMEM(mixed, bf16),) * 2,
        in_specs=[
            pl.BlockSpec(memory_space=pltpu.SMEM),
            pl.BlockSpec(memory_space=pl.ANY),
            pl.BlockSpec(memory_space=pl.ANY),
            pl.BlockSpec(memory_space=pl.ANY),
        ],
        out_specs=(pl.BlockSpec(memory_space=pltpu.VMEM),) * 2,
        scratch_shapes=[
            vmem((EXP * EXPERTS_HERE, SLOTS, WIDTH), bf16),
            vmem(mixed, bf16),
            vmem(rows, bf16),
            vmem(rows, bf16),
            vmem(rows, bf16),
            vmem((EXP, SIDES, SIDE_ROWS, WIDTH), bf16),
            vmem((SIDES, EXP, SIDE_ROWS, WIDTH), bf16),
            vmem((SIDE_EXPERTS, 2, SIDES * TOKENS, HALF), bf16),
            vmem((CHIPS, 2 * TOKENS, HALF), bf16),
            vmem((CHIPS, 2, TOKENS, HIDDEN), bf16),
            vmem(rows, bf16),
            vmem(rows, bf16),
            vmem(rows, bf16),
            vmem(rows, bf16),
            vmem(square, bf16),
            vmem(square, bf16),
            vmem(square, f32),
            vmem((8, 128), f32),
            vmem((8, 128), f32),
            vmem(square, bf16),
            vmem(square, bf16),
            vmem(square, bf16),
            vmem(square, bf16),
            vmem(square, bf16),
            vmem(square, bf16),
            dma((2, EXP)),
            dma((2, EXP)),
            dma((CHIPS,)),
            dma((CHIPS, SIDES)),
            dma((CHIPS,)),
            dma((CHIPS,)),
            dma((CHIPS,)),
            dma((CHIPS,)),
            dma((CHIPS,)),
            dma((CHIPS,)),
            dma((CHIPS,)),
            dma((CHIPS,)),
            dma((CHIPS,)),
            dma((2,)),
            dma((2,)),
            dma((8,)),
            pltpu.SemaphoreType.REGULAR,
            pltpu.SemaphoreType.REGULAR,
        ],
        compiler_params=pltpu.CompilerParams(
            collective_id=0, has_side_effects=True, vmem_limit_bytes=60 << 20
        ),
        name="muon_owner",
    )(live, tok, cot, momentum)


def solution(mesh):
    in_specs = (
        P("rep", "exp", None, None, None),
        P("rep", "exp", None, None, None),
        P("rep", "exp", None),
        P("rep", "exp", None, None),
    )
    out_specs = (P("rep", "exp", None, None), P("rep", "exp", None, None))
    return jax.shard_map(
        on_device, mesh=mesh, in_specs=in_specs, out_specs=out_specs, check_vma=False
    )
```
